32 devices in a mesh: groups: 2 (over x), gz: 16 (over z, y, core).
Axes of the slice: x: 2, y: 2, z: 4, core: 2. Of those that a mesh axis runs over, the one named last changes fastest.
Arguments:
- waves: bfloat16 [192, 8, 64, 256], P(('groups', 'gz')), parts along dimension 0, may hold values from -6 to 6
- potential: float32 [192, 512], P(('groups', 'gz')), parts along dimension 0, may hold values from 0.25 to 4
- domain_of: int32 [32], P('groups'), parts along dimension 0, may hold values from 0 to 7, never falling along the last dimension, each value on 1 to 9 neighbouring positions
Outputs:
- orbitals: bfloat16 [192, 8, 64, 256], P(('groups', 'gz')), parts along dimension 0
The draws below stay inside these ranges and needn't reach their ends.
There are 2 independent parts, one for each index of `groups`. The reference program is written for one: setup_inputs(seed, part) draws one part's arguments, and reference() takes and returns one part's arrays. A program takes and returns all parts, laid end to end along the dimension named above; each array names one. Nothing has to cross between parts.
Inputs may be any that keep to these rules, and one draw needn't show every extreme that they name: `domain_of`: never falls; every domain holds 1 to 9 blocks, one domain exactly that many.
All inputs are finite; a program needn't handle non-finite values.
Results may differ from the reference program's by a relative error of at most 0.0038.
The reference program's roundings to bfloat16 on the way count: a program that leaves them out, or rounds other values in their place, can miss the bound.
Values may be sent and summed in bfloat16 or wider, within the bound.
A program may use at most 64 MiB of HBM per device.

```python
import math
import jax
import jax.numpy as jnp
import numpy as np
from jax import lax

NB = 256
PANEL = 128
NX = 64
NY = 8
CZ = 6
DOMS = 8
DEGREE = 4
NZ = 96
N_GZ = 16


def level_of(rng, extent, cuts, low, top_value):
    level = 1.0
    for dim, parts in cuts:
        draws = jax.random.uniform(jax.random.fold_in(jax.random.fold_in(rng, 6), dim), (parts,), jnp.float32, low / len(cuts), top_value / len(cuts))
        level = level * jnp.repeat(jnp.exp(draws), extent[dim] // parts).reshape((-1,) + (1,) * (len(extent) - 1 - dim))
    return level


def split_up(amount, total, reach, slope):
    weights = [(1 << 20) // math.isqrt(standing ** slope) + 1 for standing in range(2, amount + 1)]
    spare, holding = total - reach - (amount - 1), [1] * (amount - 1)
    while spare > 0:
        free = [i for i in range(amount - 1) if holding[i] < reach]
        pool, budget = sum([weights[i] for i in free]), spare
        for i in free:
            addition = min(reach - holding[i], max(1, budget * weights[i] // pool), spare)
            holding[i] = holding[i] + addition
            spare = spare - addition
    return np.array([reach] + holding)


def uneven_parts(stream_key, amount, total, reach, slope):
    if amount == 2:
        one = jax.random.randint(stream_key, (), max(1, total - reach), min(reach, total - 1) + 1)
        return jnp.stack([one, total - one])
    sizes = jnp.asarray(split_up(amount, total, reach, slope), jnp.int32)
    couples = (amount - 1) // 2
    giver, sink = sizes[1:1 + 2 * couples:2], sizes[2:2 + 2 * couples:2]
    room = jnp.minimum(giver - 1, reach - sink)
    passed = jax.random.randint(jax.random.fold_in(stream_key, 1), (couples,), 0, 1 << 20) % (room + 1)
    sizes = sizes.at[1:1 + 2 * couples:2].set(giver - passed).at[2:2 + 2 * couples:2].set(sink + passed)
    return sizes[jax.random.permutation(jax.random.fold_in(stream_key, 2), amount)]


def scatter_about(own_key, dims, deviation, reach, shards=(), held_as=jnp.bfloat16):
    drawn = jax.random.normal(own_key, dims, jnp.float32) * deviation
    if len(shards) > 0:
        drawn = level_of(own_key, dims, shards, -0.22, 0.18) * drawn
    return jnp.clip(drawn, min=-reach, max=reach).astype(held_as)


def setup_inputs(seed: int = 0, part: int = 0) -> dict:
    key_list = jax.random.split(jax.random.key(seed), 4)
    part_splits = jax.random.split(jax.random.fold_in(key_list[3], part), 4)
    waves = scatter_about(part_splits[0], (NZ, NY, NX, NB), 1.0, 6.0, ((0, 16),))
    potential = jnp.clip(jnp.exp(math.log(4.0) - 2.7725887 * jax.random.uniform(part_splits[1], (NZ, NY * NX), jnp.float32) ** level_of(part_splits[1], (NZ, NY * NX), ((0, 16),), -0.2, 0.2)), 0.25, 4.0)
    domain_of = jnp.searchsorted(jnp.cumsum(uneven_parts(part_splits[2], DOMS, N_GZ, N_GZ // 2 + 1, 2)), jnp.arange(N_GZ), side="right").astype(jnp.int32)
    return dict(waves=waves, potential=potential, domain_of=domain_of)


COEF = (-49.0 / 18.0, 1.5, -0.15, 1.0 / 90.0)
CSHIFT = 7.0
EWIDTH = 5.0

def hamiltonian(extended, potential):
    inner = extended[3:-3]
    planes = inner.shape[0]
    rows_y = inner.shape[1]
    rows_x = inner.shape[2]
    padded_y = jnp.pad(inner, ((0, 0), (3, 3), (0, 0), (0, 0)))
    padded_x = jnp.pad(inner, ((0, 0), (0, 0), (3, 3), (0, 0)))
    total = 3.0 * COEF[0] * inner
    for distance in (1, 2, 3):
        along_z = extended[3 + distance:3 + distance + planes] + extended[3 - distance:3 - distance + planes]
        along_y = padded_y[:, 3 + distance:3 + distance + rows_y] + padded_y[:, 3 - distance:3 - distance + rows_y]
        along_x = padded_x[:, :, 3 + distance:3 + distance + rows_x] + padded_x[:, :, 3 - distance:3 - distance + rows_x]
        total = total + COEF[distance] * (along_z + along_y + along_x)
    return potential[:, :, :, None] * inner - 0.5 * total

def reference(waves, potential, domain_of):
    slabs = N_GZ
    shaped = waves.reshape(slabs, CZ, NY, NX, NB)
    grid = potential.reshape(slabs, CZ, NY, NX)
    below = jnp.concatenate([jnp.zeros((1,), jnp.float32), (domain_of[1:] == domain_of[:-1]).astype(jnp.float32)])
    above = jnp.concatenate([(domain_of[:-1] == domain_of[1:]).astype(jnp.float32), jnp.zeros((1,), jnp.float32)])
    below_mask = below[:, None, None, None, None]
    above_mask = above[:, None, None, None, None]

    def extend(field):
        zeros = jnp.zeros_like(field[:1, :3])
        lower_rim = jnp.concatenate([zeros, field[:-1, -3:]], axis=0) * below_mask
        upper_rim = jnp.concatenate([field[1:, :3], zeros], axis=0) * above_mask
        return jnp.concatenate([lower_rim, field, upper_rim], axis=1)
    apply_all = jax.vmap(hamiltonian)

    def filter_bands(block):
        field = block.astype(jnp.float32)
        image = apply_all(extend(field), grid)
        older = block
        current = ((image - CSHIFT * field) / EWIDTH).astype(jnp.bfloat16)
        for turn in range(DEGREE - 1):
            field = current.astype(jnp.float32)
            image = apply_all(extend(field), grid)
            newer = (2.0 / EWIDTH * (image - CSHIFT * field) - older.astype(jnp.float32)).astype(jnp.bfloat16)
            older, current = (current, newer)
        return current
    width = 32
    blocks = jnp.moveaxis(shaped.reshape(slabs, CZ, NY, NX, NB // width, width), 4, 0)
    filtered = lax.map(filter_bands, blocks)
    filtered = jnp.moveaxis(filtered, 0, 4).reshape(slabs, CZ * NY * NX, NB)
    picker = (domain_of[:, None] == jnp.arange(DOMS)[None, :]).astype(jnp.float32)
    cells = jnp.sum(picker, axis=0) * (CZ * NY * NX)

    def domain_mean(local):
        summed = jnp.einsum('sd,sab->dab', picker, local)
        return summed / cells[:, None, None]
    eye = jnp.eye(PANEL, dtype=jnp.float32)
    pieces = []
    for panel in range(NB // PANEL):
        block = filtered[:, :, panel * PANEL:(panel + 1) * PANEL]
        if panel > 0:
            earlier = jnp.concatenate(pieces, axis=-1)
            correlation = domain_mean(jnp.einsum('sca,scb->sab', earlier.astype(jnp.float32), block.astype(jnp.float32)))
            mine = correlation.astype(jnp.bfloat16)[domain_of]
            block = (block.astype(jnp.float32) - jnp.einsum('sca,sab->scb', earlier.astype(jnp.float32), mine.astype(jnp.float32))).astype(jnp.bfloat16)
        gram = domain_mean(jnp.einsum('sca,scb->sab', block.astype(jnp.float32), block.astype(jnp.float32)))
        factor = jnp.linalg.cholesky(gram)
        inverse = jax.vmap(lambda item: jax.scipy.linalg.solve_triangular(item, eye, lower=True))(factor)
        whitening = jnp.swapaxes(inverse, 1, 2).astype(jnp.bfloat16)[domain_of]
        pieces.append(jnp.einsum('sca,sab->scb', block.astype(jnp.float32), whitening.astype(jnp.float32)).astype(jnp.bfloat16))
    return jnp.concatenate(pieces, axis=-1).reshape(slabs * CZ, NY, NX, NB)
```

```python
import functools

import jax
import jax.numpy as jnp
import ml_dtypes
import numpy as np
from jax import lax
from jax.experimental import pallas as pl
from jax.experimental.pallas import tpu as pltpu
from jax.sharding import PartitionSpec as P

PANEL = 128
NX = 64
NY = 8
CELLS = NX * NY
DEGREE = 4
COEF = (-49.0 / 18.0, 1.5, -0.15, 1.0 / 90.0)
CSHIFT = 7.0
EWIDTH = 5.0
HALO = 3
TILE = 128
MESH = pl.DeviceIdType.MESH


def plane_matrix():
    full = np.zeros((CELLS, CELLS), np.float64)
    for y in range(NY):
        for x in range(NX):
            row = y * NX + x
            for k in (1, 2, 3):
                for s in (-k, k):
                    if 0 <= x + s < NX:
                        full[row, row + s] += -0.5 * COEF[k]
                    if 0 <= y + s < NY:
                        full[row, row + s * NX] += -0.5 * COEF[k]
    high = full.astype(ml_dtypes.bfloat16)
    low = (full - high.astype(np.float64)).astype(ml_dtypes.bfloat16)
    return np.stack([high, low])


def filter_kernel(
    n, rows, wav, pot, wz, wg, amat, fil_out, g_out,
    ext, last, potb, diag, fil, acc, gsend, grecv, gback, gfin,
    in_send, in_recv, pot_send, pot_recv, halo_send, halo_recv,
    out_send, out_recv, a_send, a_recv, b_send, b_recv,
):
    me = lax.axis_index("gz")
    planes = wav.shape[0]
    own = 2 * planes
    quad = me // 4
    r = me % 4
    half = r // 2
    core = r % 2
    link = quad * 2 + core
    lower_dev = ((link - 1) // 2) * 4 + 2 * half + (link + 1) % 2
    upper_dev = ((link + 1) // 2) * 4 + 2 * half + (link + 1) % 2
    has_lower = link > 0
    has_upper = link < n // 2 - 1

    barrier = pltpu.get_barrier_semaphore()

    @pl.loop(1, n)
    def _(off):
        pl.semaphore_signal(
            barrier, inc=1, device_id={"gz": (me + off) % n}, device_id_type=MESH
        )

    pl.semaphore_wait(barrier, n - 1)

    slot = r % 2
    starts = (HALO * slot, HALO * (1 - slot))

    def in_copy(h, piece, remote):
        start = starts[piece]
        src = wav.at[pl.ds(start, HALO), :, h * PANEL : (h + 1) * PANEL]
        dst = ext.at[0, pl.ds(HALO + planes * slot + start, HALO)]
        if remote:
            return pltpu.make_async_remote_copy(
                src_ref=src, dst_ref=dst,
                send_sem=in_send.at[h, piece], recv_sem=in_recv.at[slot, piece],
                device_id={"gz": quad * 4 + 2 * h + half}, device_id_type=MESH,
            )
        return pltpu.make_async_copy(src, dst, in_recv.at[slot, piece])

    def pot_copy(h, remote):
        if remote:
            return pltpu.make_async_remote_copy(
                src_ref=pot, dst_ref=potb.at[slot],
                send_sem=pot_send.at[h], recv_sem=pot_recv.at[slot],
                device_id={"gz": quad * 4 + 2 * h + half}, device_id_type=MESH,
            )
        return pltpu.make_async_copy(pot, potb.at[slot], pot_recv.at[slot])

    for h in (0, 1):
        away = quad * 4 + 2 * h + half != me

        @pl.when(away)
        def _(h=h):
            in_copy(h, 0, True).start()
            pot_copy(h, True).start()
            in_copy(h, 1, True).start()

        @pl.when(jnp.logical_not(away))
        def _(h=h):
            in_copy(h, 0, False).start()
            pot_copy(h, False).start()
            in_copy(h, 1, False).start()

    @pl.when(jnp.logical_not(has_lower))
    def _():
        for step in range(DEGREE):
            ext[step, 0:HALO] = jnp.zeros((HALO, CELLS, PANEL), jnp.bfloat16)

    @pl.when(jnp.logical_not(has_upper))
    def _():
        for step in range(DEGREE):
            ext[step, HALO + own : HALO + own + HALO] = jnp.zeros(
                (HALO, CELLS, PANEL), jnp.bfloat16
            )

    def in_wait(which, piece):
        start = HALO * which if piece == 0 else HALO * (1 - which)
        dst = ext.at[0, pl.ds(HALO + planes * which + start, HALO)]
        pltpu.make_async_copy(dst, dst, in_recv.at[which, piece]).wait()

    def down_copy(step):
        return pltpu.make_async_remote_copy(
            src_ref=ext.at[step, pl.ds(HALO, HALO)],
            dst_ref=ext.at[step, pl.ds(HALO + own, HALO)],
            send_sem=halo_send.at[step, 0], recv_sem=halo_recv.at[step, 0],
            device_id={"gz": lower_dev}, device_id_type=MESH,
        )

    def up_copy(step):
        return pltpu.make_async_remote_copy(
            src_ref=ext.at[step, pl.ds(own, HALO)],
            dst_ref=ext.at[step, pl.ds(0, HALO)],
            send_sem=halo_send.at[step, 1], recv_sem=halo_recv.at[step, 1],
            device_id={"gz": upper_dev}, device_id_type=MESH,
        )

    def send_halos(step):
        @pl.when(has_lower)
        def _():
            down_copy(step).start()

        @pl.when(has_upper)
        def _():
            up_copy(step).start()

    def wait_halos(step):
        @pl.when(has_upper)
        def _():
            down_copy(step).wait_recv()

        @pl.when(has_lower)
        def _():
            up_copy(step).wait_recv()

    in_wait(0, 0)
    in_wait(1, 0)
    send_halos(0)

    for which in (0, 1):
        pltpu.make_async_copy(potb.at[which], potb.at[which], pot_recv.at[which]).wait()

        @pl.loop(0, planes)
        def _(i, which=which):
            row = potb[which, pl.ds(i, 1), :] - (CSHIFT + 1.5 * COEF[0])
            diag[planes * which + i] = jnp.broadcast_to(row, (PANEL, CELLS)).T

    in_wait(0, 1)
    in_wait(1, 1)

    def update(step, first, second):
        pair = jnp.concatenate([ext[step, HALO + first], ext[step, HALO + second]], axis=1)
        for tile in range(CELLS // TILE):
            at = slice(tile * TILE, (tile + 1) * TILE)
            image = jnp.dot(
                amat[0, at, :], pair, preferred_element_type=jnp.float32
            ) + jnp.dot(amat[1, at, :], pair, preferred_element_type=jnp.float32)
            for place, plane in enumerate((first, second)):
                value = image[:, place * PANEL : (place + 1) * PANEL]
                centre = ext[step, HALO + plane, at, :].astype(jnp.float32)
                value = value + diag[plane, at, :] * centre
                for k in (1, 2, 3):
                    value = value + wz[plane, 2 * k - 2] * ext[
                        step, HALO + plane - k, at, :
                    ].astype(jnp.float32)
                    value = value + wz[plane, 2 * k - 1] * ext[
                        step, HALO + plane + k, at, :
                    ].astype(jnp.float32)
                if step == 0:
                    value = value * (1.0 / EWIDTH)
                else:
                    older = ext[step - 1, HALO + plane, at, :].astype(jnp.float32)
                    value = value * (2.0 / EWIDTH) - older
                value = value.astype(jnp.bfloat16)
                if step < DEGREE - 1:
                    ext[step + 1, HALO + plane, at, :] = value
                else:
                    last[plane, at, :] = value

    def out_copy(which, piece, remote):
        start = HALO * which if piece == 0 else HALO * (1 - which)
        src = last.at[pl.ds(planes * which + start, HALO)]
        dst = fil.at[half, pl.ds(start, HALO)]
        if remote:
            return pltpu.make_async_remote_copy(
                src_ref=src, dst_ref=dst,
                send_sem=out_send.at[which, piece], recv_sem=out_recv.at[half, piece],
                device_id={"gz": quad * 4 + 2 * core + which}, device_id_type=MESH,
            )
        return pltpu.make_async_copy(src, dst, out_recv.at[half, piece])

    def send_out(piece):
        for which in (0, 1):
            away = quad * 4 + 2 * core + which != me

            @pl.when(away)
            def _(which=which):
                out_copy(which, piece, True).start()

            @pl.when(jnp.logical_not(away))
            def _(which=which):
                out_copy(which, piece, False).start()

    for step in range(DEGREE):
        wait_halos(step)

        @pl.loop(0, HALO)
        def _(t, step=step):
            update(step, t, own - 1 - t)

        if step < DEGREE - 1:
            send_halos(step + 1)
        else:
            send_out(0)

        @pl.loop(0, HALO)
        def _(t, step=step):
            update(step, HALO + t, own - 1 - HALO - t)

    send_out(1)

    def out_wait(h, piece):
        start = HALO * slot if piece == 0 else HALO * (1 - slot)
        dst = fil.at[h, pl.ds(start, HALO)]
        pltpu.make_async_copy(dst, dst, out_recv.at[h, piece]).wait()

    for piece in (0, 1):
        for h in (0, 1):
            out_wait(h, piece)

    acc[...] = jnp.zeros_like(acc)

    @pl.loop(0, planes)
    def _(i):
        both = jnp.concatenate([fil[0, i], fil[1, i]], axis=1)
        fil_out[i] = both
        gram = lax.dot_general(
            both, both, (((0,), (0,)), ((), ())), preferred_element_type=jnp.float32
        )
        acc[0] += gram[0:PANEL, 0:PANEL]
        acc[1] += gram[0:PANEL, PANEL:]
        acc[2] += gram[PANEL:, PANEL:]

    @pl.loop(0, n)
    def _(j):
        at = pl.ds(pl.multiple_of(j * rows, rows), rows)
        gsend[j] = acc[:, at, :]

    def exchange(src, dst, send, recv):
        def copy(target, origin):
            return pltpu.make_async_remote_copy(
                src_ref=src.at[target], dst_ref=dst.at[origin],
                send_sem=send.at[target], recv_sem=recv.at[origin],
                device_id={"gz": target}, device_id_type=MESH,
            )

        @pl.loop(1, n)
        def _(off):
            copy((me + off) % n, me).start()

        dst[me] = src[me]

        @pl.loop(1, n)
        def _(off):
            copy((me + off) % n, (me + off) % n).wait_recv()

    exchange(gsend, grecv, a_send, a_recv)

    @pl.loop(0, n)
    def _(j):
        def add(i, total):
            return total + wg[j, i] * grecv[i]

        gback[j] = lax.fori_loop(0, n, add, jnp.zeros((3, rows, PANEL), jnp.float32))

    exchange(gback, gfin, b_send, b_recv)
    g_out[...] = gfin[...]

    for h in (0, 1):
        away = quad * 4 + 2 * h + half != me

        @pl.when(away)
        def _(h=h):
            in_copy(h, 0, True).wait_send()
            pot_copy(h, True).wait_send()
            in_copy(h, 1, True).wait_send()

        back = quad * 4 + 2 * core + h != me

        @pl.when(back)
        def _(h=h):
            out_copy(h, 0, True).wait_send()
            out_copy(h, 1, True).wait_send()

    for step in range(DEGREE):

        @pl.when(has_lower)
        def _(step=step):
            down_copy(step).wait_send()

        @pl.when(has_upper)
        def _(step=step):
            up_copy(step).wait_send()

    @pl.loop(1, n)
    def _(off):
        there = (me + off) % n
        pltpu.make_async_copy(gsend.at[there], gsend.at[there], a_send.at[there]).wait()
        pltpu.make_async_copy(gback.at[there], gback.at[there], b_send.at[there]).wait()


def filtered_and_gram(n, waves, potential, domain_of):
    planes = waves.shape[0]
    bands = waves.shape[2]
    rows = PANEL // n
    own = 2 * planes
    me = lax.axis_index("gz")
    base = 4 * (me // 4) + 2 * (me % 2)
    plane = jnp.arange(own)
    home = domain_of[base + plane // planes]
    columns = []
    for k in (1, 2, 3):
        for s in (-k, k):
            block = base + (plane + s + planes) // planes - 1
            inside = (block >= 0) & (block < n)
            linked = inside & (domain_of[jnp.clip(block, 0, n - 1)] == home)
            columns.append(jnp.where(linked, -0.5 * COEF[k], 0.0).astype(jnp.float32))
    wz = jnp.stack(columns, axis=1)
    same = (domain_of[:, None] == domain_of[None, :]).astype(jnp.float32)
    wg = same / (jnp.sum(same, axis=1, keepdims=True) * (planes * CELLS))
    vmem = pl.BlockSpec(memory_space=pltpu.VMEM)
    smem = pl.BlockSpec(memory_space=pltpu.SMEM)
    hbm = pl.BlockSpec(memory_space=pl.ANY)
    dma = pltpu.SemaphoreType.DMA
    chunk = pltpu.VMEM((n, 3, rows, PANEL), jnp.float32)
    return pl.pallas_call(
        functools.partial(filter_kernel, n, rows),
        out_shape=(
            jax.ShapeDtypeStruct((planes, CELLS, bands), jnp.bfloat16),
            jax.ShapeDtypeStruct((n, 3, rows, PANEL), jnp.float32),
        ),
        in_specs=[hbm, vmem, smem, smem, vmem],
        out_specs=(vmem, vmem),
        scratch_shapes=[
            pltpu.VMEM((DEGREE, own + 2 * HALO, CELLS, PANEL), jnp.bfloat16),
            pltpu.VMEM((own, CELLS, PANEL), jnp.bfloat16),
            pltpu.VMEM((2, planes, CELLS), jnp.float32),
            pltpu.VMEM((own, CELLS, PANEL), jnp.float32),
            pltpu.VMEM((2, planes, CELLS, PANEL), jnp.bfloat16),
            pltpu.VMEM((3, PANEL, PANEL), jnp.float32),
            chunk, chunk, chunk, chunk,
            dma((2, 2)), dma((2, 2)), dma((2,)), dma((2,)),
            dma((DEGREE, 2)), dma((DEGREE, 2)), dma((2, 2)), dma((2, 2)),
            dma((n,)), dma((n,)), dma((n,)), dma((n,)),
        ],
        compiler_params=pltpu.CompilerParams(
            collective_id=0, has_side_effects=True, vmem_limit_bytes=40 * 2**20
        ),
        cost_estimate=pl.CostEstimate(
            flops=8 * 10**9, bytes_accessed=5 * 10**6, transcendentals=0
        ),
        name="filter_gram",
    )(waves, potential, wz, wg, jnp.asarray(plane_matrix()))


def exact(a, b):
    return jnp.dot(a, b, precision=lax.Precision.HIGHEST, preferred_element_type=jnp.float32)


def whiten(gram):
    factor = jnp.linalg.cholesky(gram)
    inverse = jax.scipy.linalg.solve_triangular(
        factor, jnp.eye(PANEL, dtype=jnp.float32), lower=True
    )
    return inverse.T.astype(jnp.bfloat16)


def shards(waves, potential, domain_of):
    n = lax.axis_size("gz")
    planes = waves.shape[0]
    bands = waves.shape[3]
    filtered, sums = filtered_and_gram(
        n, waves.reshape(planes, CELLS, bands), potential, domain_of
    )
    sums = jnp.swapaxes(sums, 0, 1).reshape(3, PANEL, PANEL)
    g00, g01, g11 = sums[0], sums[1], sums[2]
    cells = filtered.reshape(planes * CELLS, bands)
    b0, b1 = cells[:, :PANEL], cells[:, PANEL:]
    w0 = whiten(g00)
    w0f = w0.astype(jnp.float32)
    corr = exact(w0f.T, g01)
    corr_r = corr.astype(jnp.bfloat16)
    cf = corr_r.astype(jnp.float32)
    cross = exact(cf.T, corr)
    gram1 = g11 - cross - cross.T + exact(cf.T, exact(exact(w0f.T, exact(g00, w0f)), cf))
    w1 = whiten(gram1)
    e0 = jnp.dot(b0, w0, preferred_element_type=jnp.float32).astype(jnp.bfloat16)
    reduced = (
        b1.astype(jnp.float32) - jnp.dot(e0, corr_r, preferred_element_type=jnp.float32)
    ).astype(jnp.bfloat16)
    e1 = jnp.dot(reduced, w1, preferred_element_type=jnp.float32).astype(jnp.bfloat16)
    return jnp.concatenate([e0, e1], axis=1).reshape(planes, NY, NX, bands)


def solution(mesh):
    return jax.shard_map(
        shards,
        mesh=mesh,
        in_specs=(P(("groups", "gz"), None, None, None), P(("groups", "gz"), None), P("groups")),
        out_specs=P(("groups", "gz"), None, None, None),
        check_vma=False,
    )
```

```python
import functools

import jax
import jax.numpy as jnp
import ml_dtypes
import numpy as np
from jax import lax
from jax.experimental import pallas as pl
from jax.experimental.pallas import tpu as pltpu
from jax.sharding import PartitionSpec as P

PANEL = 128
NX = 64
NY = 8
CELLS = NX * NY
DEGREE = 4
COEF = (-49.0 / 18.0, 1.5, -0.15, 1.0 / 90.0)
CSHIFT = 7.0
EWIDTH = 5.0
HALO = 3
SCALE = 2.0 / EWIDTH
TILE = 128
MESH = pl.DeviceIdType.MESH


def plane_matrix():
    full = np.zeros((CELLS, CELLS), np.float64)
    for y in range(NY):
        for x in range(NX):
            row = y * NX + x
            for k in (1, 2, 3):
                for s in (-k, k):
                    if 0 <= x + s < NX:
                        full[row, row + s] += -0.5 * SCALE * COEF[k]
                    if 0 <= y + s < NY:
                        full[row, row + s * NX] += -0.5 * SCALE * COEF[k]
    high = full.astype(ml_dtypes.bfloat16)
    low = (full - high.astype(np.float64)).astype(ml_dtypes.bfloat16)
    return np.stack([high, low])


def filter_kernel(
    n, rows, dom, wav, pot, amat, fil_out, g_out,
    wz, ext, last, potb, diag, fil, acc, gsend, grecv, gback, gfin,
    in_send, in_recv, pot_send, pot_recv, halo_send, halo_recv,
    out_send, out_recv, a_send, a_recv, b_send, b_recv,
):
    me = lax.axis_index("gz")
    planes = wav.shape[0]
    own = 2 * planes
    quad = me // 4
    r = me % 4
    half = r // 2
    core = r % 2
    link = quad * 2 + core
    lower_dev = ((link - 1) // 2) * 4 + 2 * half + (link + 1) % 2
    upper_dev = ((link + 1) // 2) * 4 + 2 * half + (link + 1) % 2
    has_lower = link > 0
    has_upper = link < n // 2 - 1

    barrier = pltpu.get_barrier_semaphore()

    @pl.loop(1, n)
    def _(off):
        pl.semaphore_signal(
            barrier, inc=1, device_id={"gz": (me + off) % n}, device_id_type=MESH
        )

    pl.semaphore_wait(barrier, n - 1)

    first = quad * 4 + core * 2
    marks = [dom[jnp.clip(first + b, 0, n - 1)] for b in (-1, 0, 1, 2)]
    ones = [
        jnp.where((marks[0] == marks[1]) & has_lower, 1.0, 0.0).astype(jnp.float32),
        jnp.where(marks[1] == marks[2], 1.0, 0.0).astype(jnp.float32),
        jnp.where((marks[2] == marks[3]) & has_upper, 1.0, 0.0).astype(jnp.float32),
    ]
    for plane in range(own):
        for k in (1, 2, 3):
            for place, other in enumerate((plane - k, plane + k)):
                a, b = plane // planes, other // planes
                weight = -0.5 * SCALE * COEF[k]
                wz[plane, 2 * k - 2 + place] = ones[max(a, b)] * weight if a != b else weight

    slot = r % 2
    starts = (HALO * slot, HALO * (1 - slot))

    def in_copy(h, piece, remote):
        start = starts[piece]
        src = wav.at[pl.ds(start, HALO), :, h * PANEL : (h + 1) * PANEL]
        dst = ext.at[0, pl.ds(HALO + planes * slot + start, HALO)]
        if remote:
            return pltpu.make_async_remote_copy(
                src_ref=src, dst_ref=dst,
                send_sem=in_send.at[h, piece], recv_sem=in_recv.at[slot, piece],
                device_id={"gz": quad * 4 + 2 * h + half}, device_id_type=MESH,
            )
        return pltpu.make_async_copy(src, dst, in_recv.at[slot, piece])

    def pot_copy(h, remote):
        if remote:
            return pltpu.make_async_remote_copy(
                src_ref=pot, dst_ref=potb.at[slot],
                send_sem=pot_send.at[h], recv_sem=pot_recv.at[slot],
                device_id={"gz": quad * 4 + 2 * h + half}, device_id_type=MESH,
            )
        return pltpu.make_async_copy(pot, potb.at[slot], pot_recv.at[slot])

    for h in (0, 1):
        away = quad * 4 + 2 * h + half != me

        @pl.when(away)
        def _(h=h):
            in_copy(h, 0, True).start()
            pot_copy(h, True).start()
            in_copy(h, 1, True).start()

        @pl.when(jnp.logical_not(away))
        def _(h=h):
            in_copy(h, 0, False).start()
            pot_copy(h, False).start()
            in_copy(h, 1, False).start()

    @pl.when(jnp.logical_not(has_lower))
    def _():
        for step in range(DEGREE):
            ext[step, 0:HALO] = jnp.zeros((HALO, CELLS, PANEL), jnp.bfloat16)

    @pl.when(jnp.logical_not(has_upper))
    def _():
        for step in range(DEGREE):
            ext[step, HALO + own : HALO + own + HALO] = jnp.zeros(
                (HALO, CELLS, PANEL), jnp.bfloat16
            )

    def in_wait(which, piece):
        start = HALO * which if piece == 0 else HALO * (1 - which)
        dst = ext.at[0, pl.ds(HALO + planes * which + start, HALO)]
        pltpu.make_async_copy(dst, dst, in_recv.at[which, piece]).wait()

    def down_copy(step):
        return pltpu.make_async_remote_copy(
            src_ref=ext.at[step, pl.ds(HALO, HALO)],
            dst_ref=ext.at[step, pl.ds(HALO + own, HALO)],
            send_sem=halo_send.at[step, 0], recv_sem=halo_recv.at[step, 0],
            device_id={"gz": lower_dev}, device_id_type=MESH,
        )

    def up_copy(step):
        return pltpu.make_async_remote_copy(
            src_ref=ext.at[step, pl.ds(own, HALO)],
            dst_ref=ext.at[step, pl.ds(0, HALO)],
            send_sem=halo_send.at[step, 1], recv_sem=halo_recv.at[step, 1],
            device_id={"gz": upper_dev}, device_id_type=MESH,
        )

    def send_halos(step):
        @pl.when(has_lower)
        def _():
            down_copy(step).start()

        @pl.when(has_upper)
        def _():
            up_copy(step).start()

    def wait_halos(step):
        @pl.when(has_upper)
        def _():
            down_copy(step).wait_recv()

        @pl.when(has_lower)
        def _():
            up_copy(step).wait_recv()

    in_wait(0, 0)
    in_wait(1, 0)
    send_halos(0)

    for which in (0, 1):
        pltpu.make_async_copy(potb.at[which], potb.at[which], pot_recv.at[which]).wait()

        @pl.loop(0, planes)
        def _(i, which=which):
            row = SCALE * (potb[which, pl.ds(i, 1), :] - (CSHIFT + 1.5 * COEF[0]))
            diag[planes * which + i] = jnp.broadcast_to(row, (PANEL, CELLS)).T

    in_wait(0, 1)
    in_wait(1, 1)

    def update(step, first, second):
        pair = jnp.concatenate([ext[step, HALO + first], ext[step, HALO + second]], axis=1)
        for tile in range(CELLS // TILE):
            at = slice(tile * TILE, (tile + 1) * TILE)
            image = jnp.dot(
                amat[0, at, :], pair, preferred_element_type=jnp.float32
            ) + jnp.dot(amat[1, at, :], pair, preferred_element_type=jnp.float32)
            for place, plane in enumerate((first, second)):
                value = image[:, place * PANEL : (place + 1) * PANEL]
                centre = ext[step, HALO + plane, at, :].astype(jnp.float32)
                value = value + diag[plane, at, :] * centre
                for k in (1, 2, 3):
                    value = value + wz[plane, 2 * k - 2] * ext[
                        step, HALO + plane - k, at, :
                    ].astype(jnp.float32)
                    value = value + wz[plane, 2 * k - 1] * ext[
                        step, HALO + plane + k, at, :
                    ].astype(jnp.float32)
                if step == 0:
                    value = value * 0.5
                else:
                    older = ext[step - 1, HALO + plane, at, :].astype(jnp.float32)
                    value = value - older
                value = value.astype(jnp.bfloat16)
                if step < DEGREE - 1:
                    ext[step + 1, HALO + plane, at, :] = value
                else:
                    last[plane, at, :] = value

    def out_copy(which, piece, remote):
        start = HALO * which if piece == 0 else HALO * (1 - which)
        src = last.at[pl.ds(planes * which + start, HALO)]
        dst = fil.at[half, pl.ds(start, HALO)]
        if remote:
            return pltpu.make_async_remote_copy(
                src_ref=src, dst_ref=dst,
                send_sem=out_send.at[which, piece], recv_sem=out_recv.at[half, piece],
                device_id={"gz": quad * 4 + 2 * core + which}, device_id_type=MESH,
            )
        return pltpu.make_async_copy(src, dst, out_recv.at[half, piece])

    def send_out(piece):
        for which in (0, 1):
            away = quad * 4 + 2 * core + which != me

            @pl.when(away)
            def _(which=which):
                out_copy(which, piece, True).start()

            @pl.when(jnp.logical_not(away))
            def _(which=which):
                out_copy(which, piece, False).start()

    for step in range(DEGREE):
        wait_halos(step)

        @pl.loop(0, HALO)
        def _(t, step=step):
            update(step, t, own - 1 - t)

        if step < DEGREE - 1:
            send_halos(step + 1)
        else:
            send_out(0)

        @pl.loop(0, HALO)
        def _(t, step=step):
            update(step, HALO + t, own - 1 - HALO - t)

    send_out(1)

    def out_wait(h, piece):
        start = HALO * slot if piece == 0 else HALO * (1 - slot)
        dst = fil.at[h, pl.ds(start, HALO)]
        pltpu.make_async_copy(dst, dst, out_recv.at[h, piece]).wait()

    for piece in (0, 1):
        for h in (0, 1):
            out_wait(h, piece)

    acc[...] = jnp.zeros_like(acc)

    @pl.loop(0, planes)
    def _(i):
        both = jnp.concatenate([fil[0, i], fil[1, i]], axis=1)
        fil_out[i] = both
        gram = lax.dot_general(
            both, both, (((0,), (0,)), ((), ())), preferred_element_type=jnp.float32
        )
        acc[0] += gram[0:PANEL, 0:PANEL]
        acc[1] += gram[0:PANEL, PANEL:]
        acc[2] += gram[PANEL:, PANEL:]

    @pl.loop(0, n)
    def _(j):
        at = pl.ds(pl.multiple_of(j * rows, rows), rows)
        gsend[j] = acc[:, at, :]

    def exchange(src, dst, send, recv):
        def copy(target, origin):
            return pltpu.make_async_remote_copy(
                src_ref=src.at[target], dst_ref=dst.at[origin],
                send_sem=send.at[target], recv_sem=recv.at[origin],
                device_id={"gz": target}, device_id_type=MESH,
            )

        @pl.loop(1, n)
        def _(off):
            copy((me + off) % n, me).start()

        dst[me] = src[me]

        @pl.loop(1, n)
        def _(off):
            copy((me + off) % n, (me + off) % n).wait_recv()

    exchange(gsend, grecv, a_send, a_recv)

    @pl.loop(0, n)
    def _(j):
        mark = dom[j]

        def add(i, sums):
            total, blocks = sums
            same = jnp.where(dom[i] == mark, 1.0, 0.0).astype(jnp.float32)
            return total + same * grecv[i], blocks + same

        zero = jnp.zeros((3, rows, PANEL), jnp.float32)
        total, blocks = lax.fori_loop(0, n, add, (zero, jnp.float32(0.0)), unroll=8)
        size = jnp.full((3, rows, PANEL), blocks * (planes * CELLS), jnp.float32)
        gback[j] = total / size

    exchange(gback, gfin, b_send, b_recv)

    @pl.loop(0, n)
    def _(j):
        g_out[:, pl.ds(pl.multiple_of(j * rows, rows), rows), :] = gfin[j]

    for h in (0, 1):
        away = quad * 4 + 2 * h + half != me

        @pl.when(away)
        def _(h=h):
            in_copy(h, 0, True).wait_send()
            pot_copy(h, True).wait_send()
            in_copy(h, 1, True).wait_send()

        back = quad * 4 + 2 * core + h != me

        @pl.when(back)
        def _(h=h):
            out_copy(h, 0, True).wait_send()
            out_copy(h, 1, True).wait_send()

    for step in range(DEGREE):

        @pl.when(has_lower)
        def _(step=step):
            down_copy(step).wait_send()

        @pl.when(has_upper)
        def _(step=step):
            up_copy(step).wait_send()

    @pl.loop(1, n)
    def _(off):
        there = (me + off) % n
        pltpu.make_async_copy(gsend.at[there], gsend.at[there], a_send.at[there]).wait()
        pltpu.make_async_copy(gback.at[there], gback.at[there], b_send.at[there]).wait()


def filtered_and_gram(n, waves, potential, domain_of):
    planes = waves.shape[0]
    bands = waves.shape[2]
    rows = PANEL // n
    own = 2 * planes
    vmem = pl.BlockSpec(memory_space=pltpu.VMEM)
    smem = pl.BlockSpec(memory_space=pltpu.SMEM)
    hbm = pl.BlockSpec(memory_space=pl.ANY)
    dma = pltpu.SemaphoreType.DMA
    chunk = pltpu.VMEM((n, 3, rows, PANEL), jnp.float32)
    return pl.pallas_call(
        functools.partial(filter_kernel, n, rows),
        out_shape=(
            jax.ShapeDtypeStruct((planes, CELLS, bands), jnp.bfloat16),
            jax.ShapeDtypeStruct((3, PANEL, PANEL), jnp.float32),
        ),
        in_specs=[smem, hbm, vmem, vmem],
        out_specs=(vmem, vmem),
        scratch_shapes=[
            pltpu.SMEM((own, 6), jnp.float32),
            pltpu.VMEM((DEGREE, own + 2 * HALO, CELLS, PANEL), jnp.bfloat16),
            pltpu.VMEM((own, CELLS, PANEL), jnp.bfloat16),
            pltpu.VMEM((2, planes, CELLS), jnp.float32),
            pltpu.VMEM((own, CELLS, PANEL), jnp.float32),
            pltpu.VMEM((2, planes, CELLS, PANEL), jnp.bfloat16),
            pltpu.VMEM((3, PANEL, PANEL), jnp.float32),
            chunk, chunk, chunk, chunk,
            dma((2, 2)), dma((2, 2)), dma((2,)), dma((2,)),
            dma((DEGREE, 2)), dma((DEGREE, 2)), dma((2, 2)), dma((2, 2)),
            dma((n,)), dma((n,)), dma((n,)), dma((n,)),
        ],
        compiler_params=pltpu.CompilerParams(
            collective_id=0, has_side_effects=True, vmem_limit_bytes=40 * 2**20
        ),
        cost_estimate=pl.CostEstimate(
            flops=8 * 10**9, bytes_accessed=5 * 10**6, transcendentals=0
        ),
        name="filter_gram",
    )(domain_of, waves, potential, jnp.asarray(plane_matrix()))


BLOCK = 8


def exact(a, b, contract=((1,), (0,))):
    return lax.dot_general(
        a, b, (contract, ((), ())),
        precision=lax.Precision.HIGHEST, preferred_element_type=jnp.float32,
    )


def inverse_factor(gram):
    row = lax.broadcasted_iota(jnp.int32, (BLOCK, PANEL), 0)
    lane = lax.broadcasted_iota(jnp.int32, (BLOCK, PANEL), 1)
    rest = gram
    result = []
    for start in range(0, PANEL, BLOCK):
        top = rest[:BLOCK]
        inside = (lane >= start) & (lane < start + BLOCK)
        pivot_columns = [
            jnp.broadcast_to(top[:, start + j : start + j + 1], (BLOCK, PANEL))
            for j in range(BLOCK)
        ]
        top = jnp.where(inside, jnp.where(lane - start == row, 1.0, 0.0), top)
        scale = jnp.zeros((BLOCK, PANEL), jnp.float32)
        for j in range(BLOCK):
            pivot = jnp.broadcast_to(pivot_columns[j][j : j + 1], (BLOCK, PANEL))
            over = 1.0 / pivot
            scale = jnp.where(row == j, over, scale)
            if j == BLOCK - 1:
                break
            factor = jnp.where(row > j, pivot_columns[j] * over, 0.0)
            for later in range(j + 1, BLOCK):
                pivot_columns[later] = pivot_columns[later] - factor * jnp.broadcast_to(
                    pivot_columns[later][j : j + 1], (BLOCK, PANEL)
                )
            top = top - factor * jnp.broadcast_to(top[j : j + 1], (BLOCK, PANEL))
        end = start + BLOCK
        result.append(jnp.where(lane < end, top * jnp.sqrt(scale), 0.0))
        if end < PANEL:
            ratio = jnp.where(lane >= end, top * scale, 0.0)
            change = exact(ratio, top, ((0,), (0,)))[end:]
            below = lax.broadcasted_iota(jnp.int32, (PANEL - end, PANEL), 1)
            keep = jnp.where((below >= start) & (below < end), 0.0, rest[BLOCK:])
            rest = keep - change
    return jnp.concatenate(result, axis=0)


def whiten_kernel(fil, sums, out):
    g00, g01, g11 = sums[0], sums[1], sums[2]
    w0 = inverse_factor(g00).astype(jnp.bfloat16)
    w0f = w0.astype(jnp.float32)
    corr = exact(w0f, g01)
    corr_r = corr.astype(jnp.bfloat16)
    cf = corr_r.astype(jnp.float32)
    middle = exact(exact(exact(w0f, g00), w0f, ((1,), (1,))), cf) - corr
    gram1 = g11 + exact(cf, middle, ((0,), (0,))) - exact(corr, cf, ((0,), (0,)))
    w1 = inverse_factor(gram1).astype(jnp.bfloat16)

    def times(a, b, contract):
        return lax.dot_general(a, b, (contract, ((), ())), preferred_element_type=jnp.float32)

    @pl.loop(0, fil.shape[0])
    def _(i):
        e0 = times(fil[i, :, :PANEL], w0, ((1,), (1,))).astype(jnp.bfloat16)
        out[i, :, :PANEL] = e0
        b1 = fil[i, :, PANEL:].astype(jnp.float32)
        reduced = (b1 - times(e0, corr_r, ((1,), (0,)))).astype(jnp.bfloat16)
        out[i, :, PANEL:] = times(reduced, w1, ((1,), (1,))).astype(jnp.bfloat16)


def shards(waves, potential, domain_of):
    n = lax.axis_size("gz")
    planes = waves.shape[0]
    bands = waves.shape[3]
    filtered, sums = filtered_and_gram(
        n, waves.reshape(planes, CELLS, bands), potential, domain_of
    )
    vmem = pl.BlockSpec(memory_space=pltpu.VMEM)
    orbitals = pl.pallas_call(
        whiten_kernel,
        out_shape=jax.ShapeDtypeStruct((planes, CELLS, bands), jnp.bfloat16),
        in_specs=[vmem, vmem],
        out_specs=vmem,
        compiler_params=pltpu.CompilerParams(vmem_limit_bytes=32 * 2**20),
        cost_estimate=pl.CostEstimate(
            flops=4 * 10**8, bytes_accessed=4 * 10**6, transcendentals=0
        ),
        name="whiten",
    )(filtered, sums)
    return orbitals.reshape(planes, NY, NX, bands)


def solution(mesh):
    return jax.shard_map(
        shards,
        mesh=mesh,
        in_specs=(P(("groups", "gz"), None, None, None), P(("groups", "gz"), None), P("groups")),
        out_specs=P(("groups", "gz"), None, None, None),
        check_vma=False,
    )
```

```python
import functools

import jax
import jax.numpy as jnp
import ml_dtypes
import numpy as np
from jax import lax
from jax.experimental import pallas as pl
from jax.experimental.pallas import tpu as pltpu
from jax.sharding import PartitionSpec as P

PANEL = 128
NX = 64
NY = 8
CELLS = NX * NY
DEGREE = 4
COEF = (-49.0 / 18.0, 1.5, -0.15, 1.0 / 90.0)
CSHIFT = 7.0
EWIDTH = 5.0
HALO = 3
SCALE = 2.0 / EWIDTH
TILE = 128
MESH = pl.DeviceIdType.MESH


def plane_matrix():
    full = np.zeros((CELLS, CELLS), np.float64)
    for y in range(NY):
        for x in range(NX):
            row = y * NX + x
            for k in (1, 2, 3):
                for s in (-k, k):
                    if 0 <= x + s < NX:
                        full[row, row + s] += -0.5 * SCALE * COEF[k]
                    if 0 <= y + s < NY:
                        full[row, row + s * NX] += -0.5 * SCALE * COEF[k]
    high = full.astype(ml_dtypes.bfloat16)
    low = (full - high.astype(np.float64)).astype(ml_dtypes.bfloat16)
    tiles = np.stack([high, low]).reshape(2, CELLS // TILE, TILE, CELLS)
    return np.swapaxes(tiles, 0, 1).reshape(CELLS // TILE, 2 * TILE, CELLS)


def filter_kernel(
    n, rows, dom, wav, pot, amat_hbm, fil_out, g_out,
    wz, amat, ext, last, potb, diag, fil, acc, gsend, grecv, gback, gfin,
    in_send, in_recv, pot_send, pot_recv, halo_send, halo_recv,
    out_send, out_recv, load, store, a_send, a_recv, b_send, b_recv,
):
    me = lax.axis_index("gz")
    planes = wav.shape[0]
    own = 2 * planes
    quad = me // 4
    r = me % 4
    half = r // 2
    core = r % 2
    link = quad * 2 + core
    lower_dev = ((link - 1) // 2) * 4 + 2 * half + (link + 1) % 2
    upper_dev = ((link + 1) // 2) * 4 + 2 * half + (link + 1) % 2
    has_lower = link > 0
    has_upper = link < n // 2 - 1

    barrier = pltpu.get_barrier_semaphore()

    @pl.loop(1, n)
    def _(off):
        pl.semaphore_signal(
            barrier, inc=1, device_id={"gz": (me + off) % n}, device_id_type=MESH
        )

    pl.semaphore_wait(barrier, n - 1)

    first = quad * 4 + core * 2
    marks = [dom[jnp.clip(first + b, 0, n - 1)] for b in (-1, 0, 1, 2)]
    ones = [
        jnp.where((marks[0] == marks[1]) & has_lower, 1.0, 0.0).astype(jnp.float32),
        jnp.where(marks[1] == marks[2], 1.0, 0.0).astype(jnp.float32),
        jnp.where((marks[2] == marks[3]) & has_upper, 1.0, 0.0).astype(jnp.float32),
    ]
    for plane in range(own):
        for k in (1, 2, 3):
            for place, other in enumerate((plane - k, plane + k)):
                a, b = plane // planes, other // planes
                weight = -0.5 * SCALE * COEF[k]
                wz[plane, 2 * k - 2 + place] = ones[max(a, b)] * weight if a != b else weight

    slot = r % 2
    starts = (HALO * slot, HALO * (1 - slot))

    def in_copy(h, piece, remote):
        start = starts[piece]
        src = wav.at[pl.ds(start, HALO), :, h * PANEL : (h + 1) * PANEL]
        dst = ext.at[0, pl.ds(HALO + planes * slot + start, HALO)]
        if remote:
            return pltpu.make_async_remote_copy(
                src_ref=src, dst_ref=dst,
                send_sem=in_send.at[h, piece], recv_sem=in_recv.at[slot, piece],
                device_id={"gz": quad * 4 + 2 * h + half}, device_id_type=MESH,
            )
        return pltpu.make_async_copy(src, dst, in_recv.at[slot, piece])

    def pot_copy(h, remote):
        if remote:
            return pltpu.make_async_remote_copy(
                src_ref=pot, dst_ref=potb.at[slot],
                send_sem=pot_send.at[h], recv_sem=pot_recv.at[slot],
                device_id={"gz": quad * 4 + 2 * h + half}, device_id_type=MESH,
            )
        return pltpu.make_async_copy(pot, potb.at[slot], pot_recv.at[slot])

    amat_copy = pltpu.make_async_copy(amat_hbm, amat, load)
    for h in (0, 1):
        away = quad * 4 + 2 * h + half != me

        @pl.when(away)
        def _(h=h):
            in_copy(h, 0, True).start()
            pot_copy(h, True).start()
            in_copy(h, 1, True).start()

        @pl.when(jnp.logical_not(away))
        def _(h=h):
            in_copy(h, 0, False).start()
            pot_copy(h, False).start()
            in_copy(h, 1, False).start()

    amat_copy.start()

    @pl.when(jnp.logical_not(has_lower))
    def _():
        for step in range(DEGREE):
            ext[step, 0:HALO] = jnp.zeros((HALO, CELLS, PANEL), jnp.bfloat16)

    @pl.when(jnp.logical_not(has_upper))
    def _():
        for step in range(DEGREE):
            ext[step, HALO + own : HALO + own + HALO] = jnp.zeros(
                (HALO, CELLS, PANEL), jnp.bfloat16
            )

    def in_wait(which, piece):
        start = HALO * which if piece == 0 else HALO * (1 - which)
        dst = ext.at[0, pl.ds(HALO + planes * which + start, HALO)]
        pltpu.make_async_copy(dst, dst, in_recv.at[which, piece]).wait()

    def down_copy(step):
        return pltpu.make_async_remote_copy(
            src_ref=ext.at[step, pl.ds(HALO, HALO)],
            dst_ref=ext.at[step, pl.ds(HALO + own, HALO)],
            send_sem=halo_send.at[step, 0], recv_sem=halo_recv.at[step, 0],
            device_id={"gz": lower_dev}, device_id_type=MESH,
        )

    def up_copy(step):
        return pltpu.make_async_remote_copy(
            src_ref=ext.at[step, pl.ds(own, HALO)],
            dst_ref=ext.at[step, pl.ds(0, HALO)],
            send_sem=halo_send.at[step, 1], recv_sem=halo_recv.at[step, 1],
            device_id={"gz": upper_dev}, device_id_type=MESH,
        )

    def send_far(step):
        @pl.when((core == 0) & has_lower)
        def _():
            down_copy(step).start()

        @pl.when((core == 1) & has_upper)
        def _():
            up_copy(step).start()

    def send_near(step):
        @pl.when(core == 0)
        def _():
            up_copy(step).start()

        @pl.when(core == 1)
        def _():
            down_copy(step).start()

    def wait_far(step):
        @pl.when((core == 0) & has_lower)
        def _():
            up_copy(step).wait_recv()

        @pl.when((core == 1) & has_upper)
        def _():
            down_copy(step).wait_recv()

    def wait_near(step):
        @pl.when(core == 0)
        def _():
            down_copy(step).wait_recv()

        @pl.when(core == 1)
        def _():
            up_copy(step).wait_recv()

    in_wait(core, 0)
    send_far(0)
    in_wait(1 - core, 0)
    send_near(0)
    amat_copy.wait()

    for which in (0, 1):
        pltpu.make_async_copy(potb.at[which], potb.at[which], pot_recv.at[which]).wait()

        @pl.loop(0, planes)
        def _(i, which=which):
            row = SCALE * (potb[which, pl.ds(i, 1), :] - (CSHIFT + 1.5 * COEF[0]))
            diag[planes * which + i] = jnp.broadcast_to(row, (PANEL, CELLS)).T

    in_wait(0, 1)
    in_wait(1, 1)

    def update(step, first, second):
        pair = jnp.concatenate([ext[step, HALO + first], ext[step, HALO + second]], axis=1)
        for tile in range(CELLS // TILE):
            at = slice(tile * TILE, (tile + 1) * TILE)
            both = jnp.dot(amat[tile], pair, preferred_element_type=jnp.float32)
            image = both[:TILE] + both[TILE:]
            for place, plane in enumerate((first, second)):
                value = image[:, place * PANEL : (place + 1) * PANEL]
                centre = ext[step, HALO + plane, at, :].astype(jnp.float32)
                value = value + diag[plane, at, :] * centre
                for k in (1, 2, 3):
                    value = value + wz[plane, 2 * k - 2] * ext[
                        step, HALO + plane - k, at, :
                    ].astype(jnp.float32)
                    value = value + wz[plane, 2 * k - 1] * ext[
                        step, HALO + plane + k, at, :
                    ].astype(jnp.float32)
                if step == 0:
                    value = value * 0.5
                else:
                    older = ext[step - 1, HALO + plane, at, :].astype(jnp.float32)
                    value = value - older
                value = value.astype(jnp.bfloat16)
                if step < DEGREE - 1:
                    ext[step + 1, HALO + plane, at, :] = value
                else:
                    last[plane, at, :] = value

    def out_copy(part, remote):
        which, piece = part // 2, part % 2
        src = last.at[pl.ds(HALO * part, HALO)]
        dst = fil.at[half, pl.ds(HALO * piece, HALO)]
        if remote:
            return pltpu.make_async_remote_copy(
                src_ref=src, dst_ref=dst,
                send_sem=out_send.at[part], recv_sem=out_recv.at[half, piece],
                device_id={"gz": quad * 4 + 2 * core + which}, device_id_type=MESH,
            )
        return pltpu.make_async_copy(src, dst, out_recv.at[half, piece])

    def send_out(t_part):
        part = jnp.where(core == 0, t_part, 3 - t_part)
        away = quad * 4 + 2 * core + part // 2 != me

        @pl.when(away)
        def _():
            out_copy(part, True).start()

        @pl.when(jnp.logical_not(away))
        def _():
            out_copy(part, False).start()

    def inward(t):
        return jnp.where(core == 0, t, own - 1 - t)

    def update_pairs(step, start, count):
        @pl.loop(0, count)
        def _(j):
            update(step, inward(start + 2 * j), inward(start + 2 * j + 1))

    for step in range(DEGREE):
        final = step == DEGREE - 1
        wait_near(step)
        update_pairs(step, own - 4, 2)
        if final:
            send_out(3)
        else:
            send_near(step + 1)
        update_pairs(step, own - 8, 2)
        if final:
            send_out(2)
        wait_far(step)
        update_pairs(step, 0, 2)
        if final:
            send_out(0)
            send_out(1)
        else:
            send_far(step + 1)

    def out_wait(h, piece):
        dst = fil.at[h, pl.ds(HALO * piece, HALO)]
        pltpu.make_async_copy(dst, dst, out_recv.at[h, piece]).wait()

    def store_copy(h, piece):
        return pltpu.make_async_copy(
            fil.at[h, pl.ds(HALO * piece, HALO)],
            fil_out.at[pl.ds(HALO * piece, HALO), :, h * PANEL : (h + 1) * PANEL],
            store.at[h, piece],
        )

    acc[...] = jnp.zeros_like(acc)
    for piece in (1 - half, half):
        for h in (0, 1):
            out_wait(h, piece)
            store_copy(h, piece).start()

        @pl.loop(0, HALO)
        def _(i, piece=piece):
            at = HALO * piece + i
            both = jnp.concatenate([fil[0, at], fil[1, at]], axis=1)
            gram = lax.dot_general(
                both, both, (((0,), (0,)), ((), ())), preferred_element_type=jnp.float32
            )
            acc[0] += gram[0:PANEL, 0:PANEL]
            acc[1] += gram[0:PANEL, PANEL:]
            acc[2] += gram[PANEL:, PANEL:]

    @pl.loop(0, n)
    def _(j):
        at = pl.ds(pl.multiple_of(j * rows, rows), rows)
        gsend[j] = acc[:, at, :]

    def exchange(src, dst, send, recv):
        def copy(target, origin):
            return pltpu.make_async_remote_copy(
                src_ref=src.at[target], dst_ref=dst.at[origin],
                send_sem=send.at[target], recv_sem=recv.at[origin],
                device_id={"gz": target}, device_id_type=MESH,
            )

        @pl.loop(1, n)
        def _(off):
            copy((me + off) % n, me).start()

        dst[me] = src[me]

        @pl.loop(1, n)
        def _(off):
            copy((me + off) % n, (me + off) % n).wait_recv()

    exchange(gsend, grecv, a_send, a_recv)

    @pl.loop(0, n)
    def _(j):
        mark = dom[j]

        def add(i, sums):
            total, blocks = sums
            same = jnp.where(dom[i] == mark, 1.0, 0.0).astype(jnp.float32)
            return total + same * grecv[i], blocks + same

        zero = jnp.zeros((3, rows, PANEL), jnp.float32)
        total, blocks = lax.fori_loop(0, n, add, (zero, jnp.float32(0.0)), unroll=8)
        size = jnp.full((3, rows, PANEL), blocks * (planes * CELLS), jnp.float32)
        gback[j] = total / size

    exchange(gback, gfin, b_send, b_recv)

    @pl.loop(0, n)
    def _(j):
        g_out[:, pl.ds(pl.multiple_of(j * rows, rows), rows), :] = gfin[j]

    for h in (0, 1):
        away = quad * 4 + 2 * h + half != me

        @pl.when(away)
        def _(h=h):
            in_copy(h, 0, True).wait_send()
            pot_copy(h, True).wait_send()
            in_copy(h, 1, True).wait_send()

        back = quad * 4 + 2 * core + h != me

        @pl.when(back)
        def _(h=h):
            out_copy(2 * h, True).wait_send()
            out_copy(2 * h + 1, True).wait_send()

        store_copy(h, 0).wait()
        store_copy(h, 1).wait()

    for step in range(DEGREE):

        @pl.when(has_lower)
        def _(step=step):
            down_copy(step).wait_send()

        @pl.when(has_upper)
        def _(step=step):
            up_copy(step).wait_send()

    @pl.loop(1, n)
    def _(off):
        there = (me + off) % n
        pltpu.make_async_copy(gsend.at[there], gsend.at[there], a_send.at[there]).wait()
        pltpu.make_async_copy(gback.at[there], gback.at[there], b_send.at[there]).wait()


def filtered_and_gram(n, waves, potential, domain_of):
    planes = waves.shape[0]
    bands = waves.shape[2]
    rows = PANEL // n
    own = 2 * planes
    vmem = pl.BlockSpec(memory_space=pltpu.VMEM)
    smem = pl.BlockSpec(memory_space=pltpu.SMEM)
    hbm = pl.BlockSpec(memory_space=pl.ANY)
    dma = pltpu.SemaphoreType.DMA
    chunk = pltpu.VMEM((n, 3, rows, PANEL), jnp.float32)
    return pl.pallas_call(
        functools.partial(filter_kernel, n, rows),
        out_shape=(
            jax.ShapeDtypeStruct((planes, CELLS, bands), jnp.bfloat16),
            jax.ShapeDtypeStruct((3, PANEL, PANEL), jnp.float32),
        ),
        in_specs=[smem, hbm, hbm, hbm],
        out_specs=(hbm, vmem),
        scratch_shapes=[
            pltpu.SMEM((own, 6), jnp.float32),
            pltpu.VMEM((CELLS // TILE, 2 * TILE, CELLS), jnp.bfloat16),
            pltpu.VMEM((DEGREE, own + 2 * HALO, CELLS, PANEL), jnp.bfloat16),
            pltpu.VMEM((own, CELLS, PANEL), jnp.bfloat16),
            pltpu.VMEM((2, planes, CELLS), jnp.float32),
            pltpu.VMEM((own, CELLS, PANEL), jnp.float32),
            pltpu.VMEM((2, planes, CELLS, PANEL), jnp.bfloat16),
            pltpu.VMEM((3, PANEL, PANEL), jnp.float32),
            chunk, chunk, chunk, chunk,
            dma((2, 2)), dma((2, 2)), dma((2,)), dma((2,)),
            dma((DEGREE, 2)), dma((DEGREE, 2)), dma((4,)), dma((2, 2)), dma, dma((2, 2)),
            dma((n,)), dma((n,)), dma((n,)), dma((n,)),
        ],
        compiler_params=pltpu.CompilerParams(
            collective_id=0, has_side_effects=True, vmem_limit_bytes=58 * 2**20
        ),
        cost_estimate=pl.CostEstimate(
            flops=8 * 10**9, bytes_accessed=5 * 10**6, transcendentals=0
        ),
        name="filter_gram",
    )(domain_of, waves, potential, jnp.asarray(plane_matrix()))


BLOCK = 8


def exact(a, b, contract=((1,), (0,))):
    return lax.dot_general(
        a, b, (contract, ((), ())),
        precision=lax.Precision.HIGHEST, preferred_element_type=jnp.float32,
    )


def inverse_factor(gram):
    row = lax.broadcasted_iota(jnp.int32, (BLOCK, PANEL), 0)
    lane = lax.broadcasted_iota(jnp.int32, (BLOCK, PANEL), 1)
    rest = gram
    result = []
    for start in range(0, PANEL, BLOCK):
        top = rest[:BLOCK]
        inside = (lane >= start) & (lane < start + BLOCK)
        pivot_columns = [
            jnp.broadcast_to(top[:, start + j : start + j + 1], (BLOCK, PANEL))
            for j in range(BLOCK)
        ]
        top = jnp.where(inside, jnp.where(lane - start == row, 1.0, 0.0), top)
        scale = jnp.zeros((BLOCK, PANEL), jnp.float32)
        for j in range(BLOCK):
            pivot = jnp.broadcast_to(pivot_columns[j][j : j + 1], (BLOCK, PANEL))
            over = 1.0 / pivot
            scale = jnp.where(row == j, over, scale)
            if j == BLOCK - 1:
                break
            factor = jnp.where(row > j, pivot_columns[j] * over, 0.0)
            for later in range(j + 1, BLOCK):
                pivot_columns[later] = pivot_columns[later] - factor * jnp.broadcast_to(
                    pivot_columns[later][j : j + 1], (BLOCK, PANEL)
                )
            top = top - factor * jnp.broadcast_to(top[j : j + 1], (BLOCK, PANEL))
        end = start + BLOCK
        result.append(jnp.where(lane < end, top * jnp.sqrt(scale), 0.0))
        if end < PANEL:
            ratio = jnp.where(lane >= end, top * scale, 0.0)
            change = exact(ratio, top, ((0,), (0,)))[end:]
            below = lax.broadcasted_iota(jnp.int32, (PANEL - end, PANEL), 1)
            keep = jnp.where((below >= start) & (below < end), 0.0, rest[BLOCK:])
            rest = keep - change
    return jnp.concatenate(result, axis=0)


def whiten_kernel(fil_hbm, sums, out_hbm, fil, out, load, store):
    load_copy = pltpu.make_async_copy(fil_hbm, fil, load)
    load_copy.start()
    g00, g01, g11 = sums[0], sums[1], sums[2]
    w0 = inverse_factor(g00).astype(jnp.bfloat16)
    w0f = w0.astype(jnp.float32)
    corr = exact(w0f, g01)
    corr_r = corr.astype(jnp.bfloat16)
    cf = corr_r.astype(jnp.float32)
    middle = exact(exact(exact(w0f, g00), w0f, ((1,), (1,))), cf) - corr
    gram1 = g11 + exact(cf, middle, ((0,), (0,))) - exact(corr, cf, ((0,), (0,)))
    w1 = inverse_factor(gram1).astype(jnp.bfloat16)

    def times(a, b, contract):
        return lax.dot_general(a, b, (contract, ((), ())), preferred_element_type=jnp.float32)

    load_copy.wait()

    @pl.loop(0, fil.shape[0])
    def _(i):
        e0 = times(fil[i, :, :PANEL], w0, ((1,), (1,))).astype(jnp.bfloat16)
        out[i, :, :PANEL] = e0
        b1 = fil[i, :, PANEL:].astype(jnp.float32)
        reduced = (b1 - times(e0, corr_r, ((1,), (0,)))).astype(jnp.bfloat16)
        out[i, :, PANEL:] = times(reduced, w1, ((1,), (1,))).astype(jnp.bfloat16)
        pltpu.make_async_copy(out.at[i], out_hbm.at[i], store.at[i]).start()

    @pl.loop(0, fil.shape[0])
    def _(i):
        pltpu.make_async_copy(out.at[i], out_hbm.at[i], store.at[i]).wait()


def shards(waves, potential, domain_of):
    n = lax.axis_size("gz")
    planes = waves.shape[0]
    bands = waves.shape[3]
    filtered, sums = filtered_and_gram(
        n, waves.reshape(planes, CELLS, bands), potential, domain_of
    )
    vmem = pl.BlockSpec(memory_space=pltpu.VMEM)
    hbm = pl.BlockSpec(memory_space=pl.ANY)
    orbitals = pl.pallas_call(
        whiten_kernel,
        out_shape=jax.ShapeDtypeStruct((planes, CELLS, bands), jnp.bfloat16),
        in_specs=[hbm, vmem],
        out_specs=hbm,
        scratch_shapes=[
            pltpu.VMEM((planes, CELLS, bands), jnp.bfloat16),
            pltpu.VMEM((planes, CELLS, bands), jnp.bfloat16),
            pltpu.SemaphoreType.DMA,
            pltpu.SemaphoreType.DMA((planes,)),
        ],
        compiler_params=pltpu.CompilerParams(vmem_limit_bytes=58 * 2**20),
        cost_estimate=pl.CostEstimate(
            flops=4 * 10**8, bytes_accessed=4 * 10**6, transcendentals=0
        ),
        name="whiten",
    )(filtered, sums)
    return orbitals.reshape(planes, NY, NX, bands)


def solution(mesh):
    return jax.shard_map(
        shards,
        mesh=mesh,
        in_specs=(P(("groups", "gz"), None, None, None), P(("groups", "gz"), None), P("groups")),
        out_specs=P(("groups", "gz"), None, None, None),
        check_vma=False,
    )
```

```python
import functools

import jax
import jax.numpy as jnp
import ml_dtypes
import numpy as np
from jax import lax
from jax.experimental import pallas as pl
from jax.experimental.pallas import tpu as pltpu
from jax.sharding import PartitionSpec as P

PANEL = 128
NX = 64
NY = 8
CELLS = NX * NY
DEGREE = 4
COEF = (-49.0 / 18.0, 1.5, -0.15, 1.0 / 90.0)
CSHIFT = 7.0
EWIDTH = 5.0
HALO = 3
SCALE = 2.0 / EWIDTH
TILE = 128
MESH = pl.DeviceIdType.MESH


def plane_matrix():
    full = np.zeros((CELLS, CELLS), np.float64)
    for y in range(NY):
        for x in range(NX):
            row = y * NX + x
            for k in (1, 2, 3):
                for s in (-k, k):
                    if 0 <= x + s < NX:
                        full[row, row + s] += -0.5 * SCALE * COEF[k]
                    if 0 <= y + s < NY:
                        full[row, row + s * NX] += -0.5 * SCALE * COEF[k]
    high = full.astype(ml_dtypes.bfloat16)
    low = (full - high.astype(np.float64)).astype(ml_dtypes.bfloat16)
    tiles = np.stack([high, low]).reshape(2, CELLS // TILE, TILE, CELLS)
    return np.swapaxes(tiles, 0, 1).reshape(CELLS // TILE, 2 * TILE, CELLS)


def filter_kernel(
    n, rows, dom, wav, pot, amat_hbm, fil_out, g_out,
    amat, ext0, ext1, ext2, ext3, last, potb, diag, fil, acc, gsend, grecv, gback, gfin,
    in_send, in_recv, pot_send, pot_recv, halo_send, halo_recv,
    out_send, out_recv, load, store, a_send, a_recv, b_send, b_recv,
):
    me = lax.axis_index("gz")
    ext = (ext0, ext1, ext2, ext3)
    planes = wav.shape[0]
    own = 2 * planes
    quad = me // 4
    r = me % 4
    half = r // 2
    core = r % 2
    link = quad * 2 + core
    lower_dev = ((link - 1) // 2) * 4 + 2 * half + (link + 1) % 2
    upper_dev = ((link + 1) // 2) * 4 + 2 * half + (link + 1) % 2
    has_lower = link > 0
    has_upper = link < n // 2 - 1

    barrier = pltpu.get_barrier_semaphore()

    @pl.loop(1, n)
    def _(off):
        pl.semaphore_signal(
            barrier, inc=1, device_id={"gz": (me + off) % n}, device_id_type=MESH
        )

    pl.semaphore_wait(barrier, n - 1)

    first = quad * 4 + core * 2
    marks = [dom[jnp.clip(first + b, 0, n - 1)] for b in (-1, 0, 1, 2)]
    ones = [
        jnp.where((marks[0] == marks[1]) & has_lower, 1.0, 0.0).astype(jnp.float32),
        jnp.where(marks[1] == marks[2], 1.0, 0.0).astype(jnp.float32),
        jnp.where((marks[2] == marks[3]) & has_upper, 1.0, 0.0).astype(jnp.float32),
    ]
    mid = ones[1]
    far = jnp.where(core == 0, ones[0], ones[2])
    near = jnp.where(core == 0, ones[2], ones[0])

    slot = r % 2
    starts = (HALO * slot, HALO * (1 - slot))

    def in_copy(h, piece, remote):
        start = starts[piece]
        src = wav.at[pl.ds(start, HALO), :, h * PANEL : (h + 1) * PANEL]
        dst = ext0.at[pl.ds(HALO + planes * slot + start, HALO)]
        if remote:
            return pltpu.make_async_remote_copy(
                src_ref=src, dst_ref=dst,
                send_sem=in_send.at[h, piece], recv_sem=in_recv.at[slot, piece],
                device_id={"gz": quad * 4 + 2 * h + half}, device_id_type=MESH,
            )
        return pltpu.make_async_copy(src, dst, in_recv.at[slot, piece])

    def pot_copy(h, remote):
        if remote:
            return pltpu.make_async_remote_copy(
                src_ref=pot, dst_ref=potb.at[slot],
                send_sem=pot_send.at[h], recv_sem=pot_recv.at[slot],
                device_id={"gz": quad * 4 + 2 * h + half}, device_id_type=MESH,
            )
        return pltpu.make_async_copy(pot, potb.at[slot], pot_recv.at[slot])

    amat_copy = pltpu.make_async_copy(amat_hbm, amat, load)
    for h in (0, 1):
        away = quad * 4 + 2 * h + half != me

        @pl.when(away)
        def _(h=h):
            in_copy(h, 0, True).start()
            pot_copy(h, True).start()
            in_copy(h, 1, True).start()

        @pl.when(jnp.logical_not(away))
        def _(h=h):
            in_copy(h, 0, False).start()
            pot_copy(h, False).start()
            in_copy(h, 1, False).start()

    amat_copy.start()

    @pl.when(jnp.logical_not(has_lower))
    def _():
        for step in range(DEGREE):
            ext[step][0:HALO] = jnp.zeros((HALO, CELLS, PANEL), jnp.bfloat16)

    @pl.when(jnp.logical_not(has_upper))
    def _():
        for step in range(DEGREE):
            ext[step][HALO + own : HALO + own + HALO] = jnp.zeros(
                (HALO, CELLS, PANEL), jnp.bfloat16
            )

    def in_wait(which, piece):
        start = HALO * which if piece == 0 else HALO * (1 - which)
        dst = ext0.at[pl.ds(HALO + planes * which + start, HALO)]
        pltpu.make_async_copy(dst, dst, in_recv.at[which, piece]).wait()

    def down_copy(step):
        return pltpu.make_async_remote_copy(
            src_ref=ext[step].at[pl.ds(HALO, HALO)],
            dst_ref=ext[step].at[pl.ds(HALO + own, HALO)],
            send_sem=halo_send.at[step, 0], recv_sem=halo_recv.at[step, 0],
            device_id={"gz": lower_dev}, device_id_type=MESH,
        )

    def up_copy(step):
        return pltpu.make_async_remote_copy(
            src_ref=ext[step].at[pl.ds(own, HALO)],
            dst_ref=ext[step].at[pl.ds(0, HALO)],
            send_sem=halo_send.at[step, 1], recv_sem=halo_recv.at[step, 1],
            device_id={"gz": upper_dev}, device_id_type=MESH,
        )

    def send_far(step):
        @pl.when((core == 0) & has_lower)
        def _():
            down_copy(step).start()

        @pl.when((core == 1) & has_upper)
        def _():
            up_copy(step).start()

    def send_near(step):
        @pl.when(core == 0)
        def _():
            up_copy(step).start()

        @pl.when(core == 1)
        def _():
            down_copy(step).start()

    def wait_far(step):
        @pl.when((core == 0) & has_lower)
        def _():
            up_copy(step).wait_recv()

        @pl.when((core == 1) & has_upper)
        def _():
            down_copy(step).wait_recv()

    def wait_near(step):
        @pl.when(core == 0)
        def _():
            down_copy(step).wait_recv()

        @pl.when(core == 1)
        def _():
            up_copy(step).wait_recv()

    in_wait(core, 0)
    send_far(0)
    in_wait(1 - core, 0)
    send_near(0)
    amat_copy.wait()

    for which in (0, 1):
        pltpu.make_async_copy(potb.at[which], potb.at[which], pot_recv.at[which]).wait()

        @pl.loop(0, planes)
        def _(i, which=which):
            row = SCALE * (potb[which, pl.ds(i, 1), :] - (CSHIFT + 1.5 * COEF[0]))
            diag[planes * which + i] = jnp.broadcast_to(row, (PANEL, CELLS)).T

    in_wait(0, 1)
    in_wait(1, 1)

    def inward(t):
        return jnp.where(core == 0, t, own - 1 - t)

    def z_terms(source, t, at):
        total = None
        for k in (1, 2, 3):
            weight = -0.5 * SCALE * COEF[k]
            outer, inner = (
                source[HALO + inward(t + s), at, :].astype(jnp.float32) for s in (-k, k)
            )
            if t - k < 0:
                term = outer * (far * weight) + inner * weight
            elif t < planes <= t + k:
                term = outer * weight + inner * (mid * weight)
            elif t - k < planes <= t:
                term = outer * (mid * weight) + inner * weight
            elif t + k >= own:
                term = outer * weight + inner * (near * weight)
            else:
                term = (outer + inner) * weight
            total = term if total is None else total + term
        return total

    def update(step, first, second):
        source = ext[step]
        pair = jnp.concatenate(
            [source[HALO + inward(first)], source[HALO + inward(second)]], axis=1
        )

        def products(tile):
            return jnp.dot(amat[tile], pair, preferred_element_type=jnp.float32)

        tiles = CELLS // TILE
        ready = products(0)
        for tile in range(tiles):
            at = slice(tile * TILE, (tile + 1) * TILE)
            both = ready
            if tile + 1 < tiles:
                ready = products(tile + 1)
            image = both[:TILE] + both[TILE:]
            for place, t in enumerate((first, second)):
                plane = inward(t)
                value = image[:, place * PANEL : (place + 1) * PANEL]
                centre = source[HALO + plane, at, :].astype(jnp.float32)
                value = value + diag[plane, at, :] * centre + z_terms(source, t, at)
                if step == 0:
                    value = value * 0.5
                else:
                    value = value - ext[step - 1][HALO + plane, at, :].astype(jnp.float32)
                value = value.astype(jnp.bfloat16)
                if step < DEGREE - 1:
                    ext[step + 1][HALO + plane, at, :] = value
                else:
                    last[plane, at, :] = value

    def out_copy(part, remote):
        which, piece = part // 2, part % 2
        src = last.at[pl.ds(HALO * part, HALO)]
        dst = fil.at[half, pl.ds(HALO * piece, HALO)]
        if remote:
            return pltpu.make_async_remote_copy(
                src_ref=src, dst_ref=dst,
                send_sem=out_send.at[part], recv_sem=out_recv.at[half, piece],
                device_id={"gz": quad * 4 + 2 * core + which}, device_id_type=MESH,
            )
        return pltpu.make_async_copy(src, dst, out_recv.at[half, piece])

    def send_out(t_part):
        part = jnp.where(core == 0, t_part, 3 - t_part)
        away = quad * 4 + 2 * core + part // 2 != me

        @pl.when(away)
        def _():
            out_copy(part, True).start()

        @pl.when(jnp.logical_not(away))
        def _():
            out_copy(part, False).start()

    def update_pairs(step, start, count):
        for j in range(count):
            update(step, start + 2 * j, start + 2 * j + 1)

    for step in range(DEGREE):
        final = step == DEGREE - 1
        wait_near(step)
        update_pairs(step, own - 4, 2)
        if final:
            send_out(3)
        else:
            send_near(step + 1)
        update_pairs(step, own - 8, 2)
        if final:
            send_out(2)
        wait_far(step)
        update_pairs(step, 0, 2)
        if final:
            send_out(0)
            send_out(1)
        else:
            send_far(step + 1)

    def out_wait(h, piece):
        dst = fil.at[h, pl.ds(HALO * piece, HALO)]
        pltpu.make_async_copy(dst, dst, out_recv.at[h, piece]).wait()

    def store_copy(h, piece):
        return pltpu.make_async_copy(
            fil.at[h, pl.ds(HALO * piece, HALO)],
            fil_out.at[pl.ds(HALO * piece, HALO), :, h * PANEL : (h + 1) * PANEL],
            store.at[h, piece],
        )

    acc[...] = jnp.zeros_like(acc)
    for piece in (1 - half, half):
        for h in (0, 1):
            out_wait(h, piece)
            store_copy(h, piece).start()

        @pl.loop(0, HALO)
        def _(i, piece=piece):
            at = HALO * piece + i
            both = jnp.concatenate([fil[0, at], fil[1, at]], axis=1)
            gram = lax.dot_general(
                both, both, (((0,), (0,)), ((), ())), preferred_element_type=jnp.float32
            )
            acc[0] += gram[0:PANEL, 0:PANEL]
            acc[1] += gram[0:PANEL, PANEL:]
            acc[2] += gram[PANEL:, PANEL:]

    @pl.loop(0, n)
    def _(j):
        at = pl.ds(pl.multiple_of(j * rows, rows), rows)
        gsend[j] = acc[:, at, :]

    def exchange(src, dst, send, recv):
        def copy(target, origin):
            return pltpu.make_async_remote_copy(
                src_ref=src.at[target], dst_ref=dst.at[origin],
                send_sem=send.at[target], recv_sem=recv.at[origin],
                device_id={"gz": target}, device_id_type=MESH,
            )

        @pl.loop(1, n)
        def _(off):
            copy((me + off) % n, me).start()

        dst[me] = src[me]

        @pl.loop(1, n)
        def _(off):
            copy((me + off) % n, (me + off) % n).wait_recv()

    exchange(gsend, grecv, a_send, a_recv)

    @pl.loop(0, n)
    def _(j):
        mark = dom[j]

        def add(i, sums):
            total, blocks = sums
            same = jnp.where(dom[i] == mark, 1.0, 0.0).astype(jnp.float32)
            return total + same * grecv[i], blocks + same

        zero = jnp.zeros((3, rows, PANEL), jnp.float32)
        total, blocks = lax.fori_loop(0, n, add, (zero, jnp.float32(0.0)), unroll=8)
        size = jnp.full((3, rows, PANEL), blocks * (planes * CELLS), jnp.float32)
        gback[j] = total / size

    exchange(gback, gfin, b_send, b_recv)

    @pl.loop(0, n)
    def _(j):
        g_out[:, pl.ds(pl.multiple_of(j * rows, rows), rows), :] = gfin[j]

    for h in (0, 1):
        away = quad * 4 + 2 * h + half != me

        @pl.when(away)
        def _(h=h):
            in_copy(h, 0, True).wait_send()
            pot_copy(h, True).wait_send()
            in_copy(h, 1, True).wait_send()

        back = quad * 4 + 2 * core + h != me

        @pl.when(back)
        def _(h=h):
            out_copy(2 * h, True).wait_send()
            out_copy(2 * h + 1, True).wait_send()

        store_copy(h, 0).wait()
        store_copy(h, 1).wait()

    for step in range(DEGREE):

        @pl.when(has_lower)
        def _(step=step):
            down_copy(step).wait_send()

        @pl.when(has_upper)
        def _(step=step):
            up_copy(step).wait_send()

    @pl.loop(1, n)
    def _(off):
        there = (me + off) % n
        pltpu.make_async_copy(gsend.at[there], gsend.at[there], a_send.at[there]).wait()
        pltpu.make_async_copy(gback.at[there], gback.at[there], b_send.at[there]).wait()


def filtered_and_gram(n, waves, potential, domain_of):
    planes = waves.shape[0]
    bands = waves.shape[2]
    rows = PANEL // n
    own = 2 * planes
    vmem = pl.BlockSpec(memory_space=pltpu.VMEM)
    smem = pl.BlockSpec(memory_space=pltpu.SMEM)
    hbm = pl.BlockSpec(memory_space=pl.ANY)
    dma = pltpu.SemaphoreType.DMA
    wide = pltpu.VMEM((own + 2 * HALO, CELLS, PANEL), jnp.bfloat16)
    chunk = pltpu.VMEM((n, 3, rows, PANEL), jnp.float32)
    return pl.pallas_call(
        functools.partial(filter_kernel, n, rows),
        out_shape=(
            jax.ShapeDtypeStruct((planes, CELLS, bands), jnp.bfloat16),
            jax.ShapeDtypeStruct((3, PANEL, PANEL), jnp.float32),
        ),
        in_specs=[smem, hbm, hbm, hbm],
        out_specs=(hbm, vmem),
        scratch_shapes=[
            pltpu.VMEM((CELLS // TILE, 2 * TILE, CELLS), jnp.bfloat16),
            wide, wide, wide, wide,
            pltpu.VMEM((own, CELLS, PANEL), jnp.bfloat16),
            pltpu.VMEM((2, planes, CELLS), jnp.float32),
            pltpu.VMEM((own, CELLS, PANEL), jnp.float32),
            pltpu.VMEM((2, planes, CELLS, PANEL), jnp.bfloat16),
            pltpu.VMEM((3, PANEL, PANEL), jnp.float32),
            chunk, chunk, chunk, chunk,
            dma((2, 2)), dma((2, 2)), dma((2,)), dma((2,)),
            dma((DEGREE, 2)), dma((DEGREE, 2)), dma((4,)), dma((2, 2)), dma, dma((2, 2)),
            dma((n,)), dma((n,)), dma((n,)), dma((n,)),
        ],
        compiler_params=pltpu.CompilerParams(
            collective_id=0, has_side_effects=True, vmem_limit_bytes=58 * 2**20
        ),
        cost_estimate=pl.CostEstimate(
            flops=8 * 10**9, bytes_accessed=5 * 10**6, transcendentals=0
        ),
        name="filter_gram",
    )(domain_of, waves, potential, jnp.asarray(plane_matrix()))


BLOCK = 8


def exact(a, b, contract=((1,), (0,))):
    return lax.dot_general(
        a, b, (contract, ((), ())),
        precision=lax.Precision.HIGHEST, preferred_element_type=jnp.float32,
    )


def inverse_factor(gram):
    row = lax.broadcasted_iota(jnp.int32, (BLOCK, PANEL), 0)
    lane = lax.broadcasted_iota(jnp.int32, (BLOCK, PANEL), 1)
    rest = gram
    result = []
    for start in range(0, PANEL, BLOCK):
        top = rest[:BLOCK]
        inside = (lane >= start) & (lane < start + BLOCK)
        pivot_columns = [
            jnp.broadcast_to(top[:, start + j : start + j + 1], (BLOCK, PANEL))
            for j in range(BLOCK)
        ]
        top = jnp.where(inside, jnp.where(lane - start == row, 1.0, 0.0), top)
        scale = jnp.zeros((BLOCK, PANEL), jnp.float32)
        for j in range(BLOCK):
            pivot = jnp.broadcast_to(pivot_columns[j][j : j + 1], (BLOCK, PANEL))
            over = 1.0 / pivot
            scale = jnp.where(row == j, over, scale)
            if j == BLOCK - 1:
                break
            column = jnp.where(row > j, pivot_columns[j], 0.0)
            for later in range(j + 1, BLOCK):
                product = column * jnp.broadcast_to(
                    pivot_columns[later][j : j + 1], (BLOCK, PANEL)
                )
                pivot_columns[later] = pivot_columns[later] - product * over
            top = top - (column * jnp.broadcast_to(top[j : j + 1], (BLOCK, PANEL))) * over
        end = start + BLOCK
        result.append(jnp.where(lane < end, top * jnp.sqrt(scale), 0.0))
        if end < PANEL:
            ratio = jnp.where(lane >= end, top * scale, 0.0)
            change = exact(ratio, top, ((0,), (0,)))[end:]
            below = lax.broadcasted_iota(jnp.int32, (PANEL - end, PANEL), 1)
            keep = jnp.where((below >= start) & (below < end), 0.0, rest[BLOCK:])
            rest = keep - change
    return jnp.concatenate(result, axis=0)


def whiten_kernel(fil_hbm, sums, out_hbm, fil, out, load, store):
    load_copy = pltpu.make_async_copy(fil_hbm, fil, load)
    load_copy.start()
    g00, g01, g11 = sums[0], sums[1], sums[2]
    w0 = inverse_factor(g00).astype(jnp.bfloat16)
    w0f = w0.astype(jnp.float32)
    corr = exact(w0f, g01)
    corr_r = corr.astype(jnp.bfloat16)
    cf = corr_r.astype(jnp.float32)
    middle = exact(exact(exact(w0f, g00), w0f, ((1,), (1,))), cf) - corr
    gram1 = g11 + exact(cf, middle, ((0,), (0,))) - exact(corr, cf, ((0,), (0,)))
    w1 = inverse_factor(gram1).astype(jnp.bfloat16)

    def times(a, b, contract):
        return lax.dot_general(a, b, (contract, ((), ())), preferred_element_type=jnp.float32)

    load_copy.wait()

    @pl.loop(0, fil.shape[0])
    def _(i):
        e0 = times(fil[i, :, :PANEL], w0, ((1,), (1,))).astype(jnp.bfloat16)
        out[i, :, :PANEL] = e0
        b1 = fil[i, :, PANEL:].astype(jnp.float32)
        reduced = (b1 - times(e0, corr_r, ((1,), (0,)))).astype(jnp.bfloat16)
        out[i, :, PANEL:] = times(reduced, w1, ((1,), (1,))).astype(jnp.bfloat16)
        pltpu.make_async_copy(out.at[i], out_hbm.at[i], store.at[i]).start()

    @pl.loop(0, fil.shape[0])
    def _(i):
        pltpu.make_async_copy(out.at[i], out_hbm.at[i], store.at[i]).wait()


def shards(waves, potential, domain_of):
    n = lax.axis_size("gz")
    planes = waves.shape[0]
    bands = waves.shape[3]
    filtered, sums = filtered_and_gram(
        n, waves.reshape(planes, CELLS, bands), potential, domain_of
    )
    vmem = pl.BlockSpec(memory_space=pltpu.VMEM)
    hbm = pl.BlockSpec(memory_space=pl.ANY)
    orbitals = pl.pallas_call(
        whiten_kernel,
        out_shape=jax.ShapeDtypeStruct((planes, CELLS, bands), jnp.bfloat16),
        in_specs=[hbm, vmem],
        out_specs=hbm,
        scratch_shapes=[
            pltpu.VMEM((planes, CELLS, bands), jnp.bfloat16),
            pltpu.VMEM((planes, CELLS, bands), jnp.bfloat16),
            pltpu.SemaphoreType.DMA,
            pltpu.SemaphoreType.DMA((planes,)),
        ],
        compiler_params=pltpu.CompilerParams(vmem_limit_bytes=58 * 2**20),
        cost_estimate=pl.CostEstimate(
            flops=4 * 10**8, bytes_accessed=4 * 10**6, transcendentals=0
        ),
        name="whiten",
    )(filtered, sums)
    return orbitals.reshape(planes, NY, NX, bands)


def solution(mesh):
    return jax.shard_map(
        shards,
        mesh=mesh,
        in_specs=(P(("groups", "gz"), None, None, None), P(("groups", "gz"), None), P("groups")),
        out_specs=P(("groups", "gz"), None, None, None),
        check_vma=False,
    )
```

```python
import functools

import jax
import jax.numpy as jnp
import ml_dtypes
import numpy as np
from jax import lax
from jax.experimental import pallas as pl
from jax.experimental.pallas import tpu as pltpu
from jax.sharding import PartitionSpec as P

PANEL = 128
NX = 64
NY = 8
CELLS = NX * NY
DEGREE = 4
COEF = (-49.0 / 18.0, 1.5, -0.15, 1.0 / 90.0)
CSHIFT = 7.0
EWIDTH = 5.0
HALO = 3
SCALE = 2.0 / EWIDTH
TILE = 128
MESH = pl.DeviceIdType.MESH


def plane_matrix():
    full = np.zeros((CELLS, CELLS), np.float64)
    for y in range(NY):
        for x in range(NX):
            row = y * NX + x
            for k in (1, 2, 3):
                for s in (-k, k):
                    if 0 <= x + s < NX:
                        full[row, row + s] += -0.5 * SCALE * COEF[k]
                    if 0 <= y + s < NY:
                        full[row, row + s * NX] += -0.5 * SCALE * COEF[k]
    high = full.astype(ml_dtypes.bfloat16)
    low = (full - high.astype(np.float64)).astype(ml_dtypes.bfloat16)
    tiles = np.stack([high, low]).reshape(2, CELLS // TILE, TILE, CELLS)
    return np.swapaxes(tiles, 0, 1).reshape(CELLS // TILE, 2 * TILE, CELLS)


def filter_kernel(
    n, rows, dom, wav, pot, amat_hbm, fil_out, g_out,
    amat, ext0, ext1, ext2, ext3, last, potb, diag, fil, acc, gsend, grecv, gback, gfin,
    in_send, in_recv, pot_send, pot_recv, halo_send, halo_recv,
    out_send, out_recv, load, store, a_send, a_recv, b_send, b_recv,
):
    me = lax.axis_index("gz")
    ext = (ext0, ext1, ext2, ext3)
    planes = wav.shape[0]
    own = 2 * planes
    quad = me // 4
    r = me % 4
    half = r // 2
    core = r % 2
    link = quad * 2 + core
    lower_dev = ((link - 1) // 2) * 4 + 2 * half + (link + 1) % 2
    upper_dev = ((link + 1) // 2) * 4 + 2 * half + (link + 1) % 2
    has_lower = link > 0
    has_upper = link < n // 2 - 1

    barrier = pltpu.get_barrier_semaphore()

    @pl.loop(1, n)
    def _(off):
        pl.semaphore_signal(
            barrier, inc=1, device_id={"gz": (me + off) % n}, device_id_type=MESH
        )

    amat_copy = pltpu.make_async_copy(amat_hbm, amat, load)
    amat_copy.start()

    @pl.when(jnp.logical_not(has_lower))
    def _():
        for step in range(DEGREE):
            ext[step][0:HALO] = jnp.zeros((HALO, CELLS, PANEL), jnp.bfloat16)

    @pl.when(jnp.logical_not(has_upper))
    def _():
        for step in range(DEGREE):
            ext[step][HALO + own : HALO + own + HALO] = jnp.zeros(
                (HALO, CELLS, PANEL), jnp.bfloat16
            )

    pl.semaphore_wait(barrier, n - 1)

    first = quad * 4 + core * 2
    marks = [dom[jnp.clip(first + b, 0, n - 1)] for b in (-1, 0, 1, 2)]
    ones = [
        jnp.where((marks[0] == marks[1]) & has_lower, 1.0, 0.0).astype(jnp.float32),
        jnp.where(marks[1] == marks[2], 1.0, 0.0).astype(jnp.float32),
        jnp.where((marks[2] == marks[3]) & has_upper, 1.0, 0.0).astype(jnp.float32),
    ]
    mid = ones[1]
    far = jnp.where(core == 0, ones[0], ones[2])
    near = jnp.where(core == 0, ones[2], ones[0])

    slot = r % 2
    starts = (HALO * slot, HALO * (1 - slot))

    def in_copy(h, piece, remote):
        start = starts[piece]
        src = wav.at[pl.ds(start, HALO), :, h * PANEL : (h + 1) * PANEL]
        dst = ext0.at[pl.ds(HALO + planes * slot + start, HALO)]
        if remote:
            return pltpu.make_async_remote_copy(
                src_ref=src, dst_ref=dst,
                send_sem=in_send.at[h, piece], recv_sem=in_recv.at[slot, piece],
                device_id={"gz": quad * 4 + 2 * h + half}, device_id_type=MESH,
            )
        return pltpu.make_async_copy(src, dst, in_recv.at[slot, piece])

    def pot_copy(h, remote):
        if remote:
            return pltpu.make_async_remote_copy(
                src_ref=pot, dst_ref=potb.at[slot],
                send_sem=pot_send.at[h], recv_sem=pot_recv.at[slot],
                device_id={"gz": quad * 4 + 2 * h + half}, device_id_type=MESH,
            )
        return pltpu.make_async_copy(pot, potb.at[slot], pot_recv.at[slot])

    for h in (0, 1):
        away = quad * 4 + 2 * h + half != me

        @pl.when(away)
        def _(h=h):
            in_copy(h, 0, True).start()
            pot_copy(h, True).start()
            in_copy(h, 1, True).start()

        @pl.when(jnp.logical_not(away))
        def _(h=h):
            in_copy(h, 0, False).start()
            pot_copy(h, False).start()
            in_copy(h, 1, False).start()

    def in_wait(which, piece):
        start = HALO * which if piece == 0 else HALO * (1 - which)
        dst = ext0.at[pl.ds(HALO + planes * which + start, HALO)]
        pltpu.make_async_copy(dst, dst, in_recv.at[which, piece]).wait()

    def down_copy(step):
        return pltpu.make_async_remote_copy(
            src_ref=ext[step].at[pl.ds(HALO, HALO)],
            dst_ref=ext[step].at[pl.ds(HALO + own, HALO)],
            send_sem=halo_send.at[step, 0], recv_sem=halo_recv.at[step, 0],
            device_id={"gz": lower_dev}, device_id_type=MESH,
        )

    def up_copy(step):
        return pltpu.make_async_remote_copy(
            src_ref=ext[step].at[pl.ds(own, HALO)],
            dst_ref=ext[step].at[pl.ds(0, HALO)],
            send_sem=halo_send.at[step, 1], recv_sem=halo_recv.at[step, 1],
            device_id={"gz": upper_dev}, device_id_type=MESH,
        )

    def send_far(step):
        @pl.when((core == 0) & has_lower)
        def _():
            down_copy(step).start()

        @pl.when((core == 1) & has_upper)
        def _():
            up_copy(step).start()

    def send_near(step):
        @pl.when(core == 0)
        def _():
            up_copy(step).start()

        @pl.when(core == 1)
        def _():
            down_copy(step).start()

    def wait_far(step):
        @pl.when((core == 0) & has_lower)
        def _():
            up_copy(step).wait_recv()

        @pl.when((core == 1) & has_upper)
        def _():
            down_copy(step).wait_recv()

    def wait_near(step):
        @pl.when(core == 0)
        def _():
            down_copy(step).wait_recv()

        @pl.when(core == 1)
        def _():
            up_copy(step).wait_recv()

    in_wait(core, 0)
    send_far(0)
    in_wait(1 - core, 0)
    send_near(0)
    amat_copy.wait()

    for which in (0, 1):
        pltpu.make_async_copy(potb.at[which], potb.at[which], pot_recv.at[which]).wait()

        @pl.loop(0, planes)
        def _(i, which=which):
            row = SCALE * (potb[which, pl.ds(i, 1), :] - (CSHIFT + 1.5 * COEF[0]))
            diag[planes * which + i] = jnp.broadcast_to(row, (PANEL, CELLS)).T

    in_wait(0, 1)
    in_wait(1, 1)

    def inward(t):
        return jnp.where(core == 0, t, own - 1 - t)

    def z_terms(source, t, at):
        total = None
        for k in (1, 2, 3):
            weight = -0.5 * SCALE * COEF[k]
            outer, inner = (
                source[HALO + inward(t + s), at, :].astype(jnp.float32) for s in (-k, k)
            )
            if t - k < 0:
                term = outer * (far * weight) + inner * weight
            elif t < planes <= t + k:
                term = outer * weight + inner * (mid * weight)
            elif t - k < planes <= t:
                term = outer * (mid * weight) + inner * weight
            elif t + k >= own:
                term = outer * weight + inner * (near * weight)
            else:
                term = (outer + inner) * weight
            total = term if total is None else total + term
        return total

    def update(step, first, second):
        source = ext[step]
        pair = jnp.concatenate(
            [source[HALO + inward(first)], source[HALO + inward(second)]], axis=1
        )

        def products(tile):
            return jnp.dot(amat[tile], pair, preferred_element_type=jnp.float32)

        tiles = CELLS // TILE
        ready = products(0)
        for tile in range(tiles):
            at = slice(tile * TILE, (tile + 1) * TILE)
            both = ready
            if tile + 1 < tiles:
                ready = products(tile + 1)
            image = both[:TILE] + both[TILE:]
            for place, t in enumerate((first, second)):
                plane = inward(t)
                value = image[:, place * PANEL : (place + 1) * PANEL]
                centre = source[HALO + plane, at, :].astype(jnp.float32)
                value = value + diag[plane, at, :] * centre + z_terms(source, t, at)
                if step == 0:
                    value = value * 0.5
                else:
                    value = value - ext[step - 1][HALO + plane, at, :].astype(jnp.float32)
                value = value.astype(jnp.bfloat16)
                if step < DEGREE - 1:
                    ext[step + 1][HALO + plane, at, :] = value
                else:
                    last[plane, at, :] = value

    def out_copy(part, remote):
        which, piece = part // 2, part % 2
        src = last.at[pl.ds(HALO * part, HALO)]
        dst = fil.at[half, pl.ds(HALO * piece, HALO)]
        if remote:
            return pltpu.make_async_remote_copy(
                src_ref=src, dst_ref=dst,
                send_sem=out_send.at[part], recv_sem=out_recv.at[half, piece],
                device_id={"gz": quad * 4 + 2 * core + which}, device_id_type=MESH,
            )
        return pltpu.make_async_copy(src, dst, out_recv.at[half, piece])

    def send_out(t_part):
        part = jnp.where(core == 0, t_part, 3 - t_part)
        away = quad * 4 + 2 * core + part // 2 != me

        @pl.when(away)
        def _():
            out_copy(part, True).start()

        @pl.when(jnp.logical_not(away))
        def _():
            out_copy(part, False).start()

    def update_pairs(step, start, count):
        for j in range(count):
            update(step, start + 2 * j, start + 2 * j + 1)

    for step in range(DEGREE):
        final = step == DEGREE - 1
        wait_near(step)
        update_pairs(step, own - 4, 2)
        if final:
            send_out(3)
        else:
            send_near(step + 1)
        update_pairs(step, own - 8, 2)
        if final:
            send_out(2)
        wait_far(step)
        update_pairs(step, 0, 2)
        if final:
            send_out(0)
            send_out(1)
        else:
            send_far(step + 1)

    def out_wait(h, piece):
        dst = fil.at[h, pl.ds(HALO * piece, HALO)]
        pltpu.make_async_copy(dst, dst, out_recv.at[h, piece]).wait()

    def store_copy(h, piece):
        return pltpu.make_async_copy(
            fil.at[h, pl.ds(HALO * piece, HALO)],
            fil_out.at[pl.ds(HALO * piece, HALO), :, h * PANEL : (h + 1) * PANEL],
            store.at[h, piece],
        )

    acc[...] = jnp.zeros_like(acc)
    for piece in (1 - half, half):
        for h in (0, 1):
            out_wait(h, piece)
            store_copy(h, piece).start()

        @pl.loop(0, HALO)
        def _(i, piece=piece):
            at = HALO * piece + i
            both = jnp.concatenate([fil[0, at], fil[1, at]], axis=1)
            gram = lax.dot_general(
                both, both, (((0,), (0,)), ((), ())), preferred_element_type=jnp.float32
            )
            acc[0] += gram[0:PANEL, 0:PANEL]
            acc[1] += gram[0:PANEL, PANEL:]
            acc[2] += gram[PANEL:, PANEL:]

    def exchange(make, src, dst, send, recv):
        def copy(target, origin):
            return pltpu.make_async_remote_copy(
                src_ref=src.at[target], dst_ref=dst.at[origin],
                send_sem=send.at[target], recv_sem=recv.at[origin],
                device_id={"gz": target}, device_id_type=MESH,
            )

        @pl.loop(1, n)
        def _(off):
            there = (me + off) % n
            src[there] = make(there)
            copy(there, me).start()

        dst[me] = make(me)

        @pl.loop(1, n)
        def _(off):
            copy((me + off) % n, (me + off) % n).wait_recv()

    def row_chunk(j):
        return acc[:, pl.ds(pl.multiple_of(j * rows, rows), rows), :]

    def domain_mean(j):
        mark = dom[j]

        def add(i, sums):
            total, blocks = sums
            same = jnp.where(dom[i] == mark, 1.0, 0.0).astype(jnp.float32)
            return total + same * grecv[i], blocks + same

        zero = jnp.zeros((3, rows, PANEL), jnp.float32)
        total, blocks = lax.fori_loop(
            0, n, add, (zero, jnp.float32(0.0)), unroll=min(n, 16)
        )
        return total / jnp.full((3, rows, PANEL), blocks * (planes * CELLS), jnp.float32)

    exchange(row_chunk, gsend, grecv, a_send, a_recv)
    exchange(domain_mean, gback, gfin, b_send, b_recv)

    @pl.loop(0, n)
    def _(j):
        g_out[:, pl.ds(pl.multiple_of(j * rows, rows), rows), :] = gfin[j]

    for h in (0, 1):
        away = quad * 4 + 2 * h + half != me

        @pl.when(away)
        def _(h=h):
            in_copy(h, 0, True).wait_send()
            pot_copy(h, True).wait_send()
            in_copy(h, 1, True).wait_send()

        back = quad * 4 + 2 * core + h != me

        @pl.when(back)
        def _(h=h):
            out_copy(2 * h, True).wait_send()
            out_copy(2 * h + 1, True).wait_send()

        store_copy(h, 0).wait()
        store_copy(h, 1).wait()

    for step in range(DEGREE):

        @pl.when(has_lower)
        def _(step=step):
            down_copy(step).wait_send()

        @pl.when(has_upper)
        def _(step=step):
            up_copy(step).wait_send()

    @pl.loop(1, n)
    def _(off):
        there = (me + off) % n
        pltpu.make_async_copy(gsend.at[there], gsend.at[there], a_send.at[there]).wait()
        pltpu.make_async_copy(gback.at[there], gback.at[there], b_send.at[there]).wait()


def filtered_and_gram(n, waves, potential, domain_of):
    planes = waves.shape[0]
    bands = waves.shape[2]
    rows = PANEL // n
    own = 2 * planes
    vmem = pl.BlockSpec(memory_space=pltpu.VMEM)
    smem = pl.BlockSpec(memory_space=pltpu.SMEM)
    hbm = pl.BlockSpec(memory_space=pl.ANY)
    dma = pltpu.SemaphoreType.DMA
    wide = pltpu.VMEM((own + 2 * HALO, CELLS, PANEL), jnp.bfloat16)
    chunk = pltpu.VMEM((n, 3, rows, PANEL), jnp.float32)
    return pl.pallas_call(
        functools.partial(filter_kernel, n, rows),
        out_shape=(
            jax.ShapeDtypeStruct((planes, CELLS, bands), jnp.bfloat16),
            jax.ShapeDtypeStruct((3, PANEL, PANEL), jnp.float32),
        ),
        in_specs=[smem, hbm, hbm, hbm],
        out_specs=(hbm, vmem),
        scratch_shapes=[
            pltpu.VMEM((CELLS // TILE, 2 * TILE, CELLS), jnp.bfloat16),
            wide, wide, wide, wide,
            pltpu.VMEM((own, CELLS, PANEL), jnp.bfloat16),
            pltpu.VMEM((2, planes, CELLS), jnp.float32),
            pltpu.VMEM((own, CELLS, PANEL), jnp.float32),
            pltpu.VMEM((2, planes, CELLS, PANEL), jnp.bfloat16),
            pltpu.VMEM((3, PANEL, PANEL), jnp.float32),
            chunk, chunk, chunk, chunk,
            dma((2, 2)), dma((2, 2)), dma((2,)), dma((2,)),
            dma((DEGREE, 2)), dma((DEGREE, 2)), dma((4,)), dma((2, 2)), dma, dma((2, 2)),
            dma((n,)), dma((n,)), dma((n,)), dma((n,)),
        ],
        compiler_params=pltpu.CompilerParams(
            collective_id=0, has_side_effects=True, vmem_limit_bytes=58 * 2**20
        ),
        cost_estimate=pl.CostEstimate(
            flops=8 * 10**9, bytes_accessed=5 * 10**6, transcendentals=0
        ),
        name="filter_gram",
    )(domain_of, waves, potential, jnp.asarray(plane_matrix()))


BLOCK = 16


def exact(a, b, contract=((1,), (0,))):
    return lax.dot_general(
        a, b, (contract, ((), ())),
        precision=lax.Precision.HIGHEST, preferred_element_type=jnp.float32,
    )


def inverse_factor(gram, beside=None):
    row = lax.broadcasted_iota(jnp.int32, (BLOCK, PANEL), 0)
    lane = lax.broadcasted_iota(jnp.int32, (BLOCK, PANEL), 1)
    rest = gram
    result = []
    for start in range(0, PANEL, BLOCK):
        if beside is not None:
            beside(start // BLOCK, PANEL // BLOCK)
        top = rest[:BLOCK]
        inside = (lane >= start) & (lane < start + BLOCK)
        pivot_columns = [
            jnp.broadcast_to(top[:, start + j : start + j + 1], (BLOCK, PANEL))
            for j in range(BLOCK)
        ]
        top = jnp.where(inside, jnp.where(lane - start == row, 1.0, 0.0), top)
        scale = jnp.zeros((BLOCK, PANEL), jnp.float32)
        for j in range(BLOCK):
            pivot = jnp.broadcast_to(pivot_columns[j][j : j + 1], (BLOCK, PANEL))
            over = 1.0 / pivot
            scale = jnp.where(row == j, over, scale)
            if j == BLOCK - 1:
                break
            column = jnp.where(row > j, pivot_columns[j], 0.0)
            for later in range(j + 1, BLOCK):
                product = column * jnp.broadcast_to(
                    pivot_columns[later][j : j + 1], (BLOCK, PANEL)
                )
                pivot_columns[later] = pivot_columns[later] - product * over
            top = top - (column * jnp.broadcast_to(top[j : j + 1], (BLOCK, PANEL))) * over
        end = start + BLOCK
        result.append(jnp.where(lane < end, top * jnp.sqrt(scale), 0.0))
        if end < PANEL:
            ratio = jnp.where(lane >= end, top * scale, 0.0)
            change = exact(ratio, top, ((0,), (0,)))[end:]
            below = lax.broadcasted_iota(jnp.int32, (PANEL - end, PANEL), 1)
            keep = jnp.where((below >= start) & (below < end), 0.0, rest[BLOCK:])
            rest = keep - change
    return jnp.concatenate(result, axis=0)


def whiten_kernel(fil_hbm, sums, out_hbm, fil, out, reduced, load, store):
    load_copy = pltpu.make_async_copy(fil_hbm, fil, load)
    load_copy.start()
    g00, g01, g11 = sums[0], sums[1], sums[2]
    w0 = inverse_factor(g00).astype(jnp.bfloat16)
    w0f = w0.astype(jnp.float32)
    corr = exact(w0f, g01)
    corr_r = corr.astype(jnp.bfloat16)
    cf = corr_r.astype(jnp.float32)
    middle = exact(exact(exact(w0f, g00), w0f, ((1,), (1,))), cf) - corr
    gram1 = g11 + exact(cf, middle, ((0,), (0,))) - exact(corr, cf, ((0,), (0,)))
    load_copy.wait()
    planes = fil.shape[0]

    def times(a, b, contract):
        return lax.dot_general(a, b, (contract, ((), ())), preferred_element_type=jnp.float32)

    chunks = [(i, t * TILE) for i in range(planes) for t in range(CELLS // TILE)]

    def reduce_some(place, blocks):
        share = -(-len(chunks) // blocks)
        for i, start in chunks[place * share : (place + 1) * share]:
            at = slice(start, start + TILE)
            e0 = times(fil[i, at, :PANEL], w0, ((1,), (1,))).astype(jnp.bfloat16)
            out[i, at, :PANEL] = e0
            b1 = fil[i, at, PANEL:].astype(jnp.float32)
            left = (b1 - times(e0, corr_r, ((1,), (0,)))).astype(jnp.bfloat16)
            reduced[i, at, :] = left

    w1 = inverse_factor(gram1, reduce_some).astype(jnp.bfloat16)

    @pl.loop(0, planes)
    def _(i):
        out[i, :, PANEL:] = times(reduced[i], w1, ((1,), (1,))).astype(jnp.bfloat16)
        pltpu.make_async_copy(out.at[i], out_hbm.at[i], store.at[i]).start()

    @pl.loop(0, fil.shape[0])
    def _(i):
        pltpu.make_async_copy(out.at[i], out_hbm.at[i], store.at[i]).wait()


def shards(waves, potential, domain_of):
    n = lax.axis_size("gz")
    planes = waves.shape[0]
    bands = waves.shape[3]
    filtered, sums = filtered_and_gram(
        n, waves.reshape(planes, CELLS, bands), potential, domain_of
    )
    vmem = pl.BlockSpec(memory_space=pltpu.VMEM)
    hbm = pl.BlockSpec(memory_space=pl.ANY)
    orbitals = pl.pallas_call(
        whiten_kernel,
        out_shape=jax.ShapeDtypeStruct((planes, CELLS, bands), jnp.bfloat16),
        in_specs=[hbm, vmem],
        out_specs=hbm,
        scratch_shapes=[
            pltpu.VMEM((planes, CELLS, bands), jnp.bfloat16),
            pltpu.VMEM((planes, CELLS, bands), jnp.bfloat16),
            pltpu.VMEM((planes, CELLS, PANEL), jnp.bfloat16),
            pltpu.SemaphoreType.DMA,
            pltpu.SemaphoreType.DMA((planes,)),
        ],
        compiler_params=pltpu.CompilerParams(vmem_limit_bytes=58 * 2**20),
        cost_estimate=pl.CostEstimate(
            flops=4 * 10**8, bytes_accessed=4 * 10**6, transcendentals=0
        ),
        name="whiten",
    )(filtered, sums)
    return orbitals.reshape(planes, NY, NX, bands)


def solution(mesh):
    return jax.shard_map(
        shards,
        mesh=mesh,
        in_specs=(P(("groups", "gz"), None, None, None), P(("groups", "gz"), None), P("groups")),
        out_specs=P(("groups", "gz"), None, None, None),
        check_vma=False,
    )
```

```python
import functools

import jax
import jax.numpy as jnp
import ml_dtypes
import numpy as np
from jax import lax
from jax.experimental import pallas as pl
from jax.experimental.pallas import tpu as pltpu
from jax.sharding import PartitionSpec as P

PANEL = 128
NX = 64
NY = 8
CELLS = NX * NY
DEGREE = 4
COEF = (-49.0 / 18.0, 1.5, -0.15, 1.0 / 90.0)
CSHIFT = 7.0
EWIDTH = 5.0
HALO = 3
SCALE = 2.0 / EWIDTH
TILE = 128
MESH = pl.DeviceIdType.MESH


def plane_matrix():
    full = np.zeros((CELLS, CELLS), np.float64)
    for y in range(NY):
        for x in range(NX):
            row = y * NX + x
            for k in (1, 2, 3):
                for s in (-k, k):
                    if 0 <= x + s < NX:
                        full[row, row + s] += -0.5 * SCALE * COEF[k]
                    if 0 <= y + s < NY:
                        full[row, row + s * NX] += -0.5 * SCALE * COEF[k]
    high = full.astype(ml_dtypes.bfloat16)
    low = (full - high.astype(np.float64)).astype(ml_dtypes.bfloat16)
    tiles = np.stack([high, low]).reshape(2, CELLS // TILE, TILE, CELLS)
    return np.swapaxes(tiles, 0, 1).reshape(CELLS // TILE, 2 * TILE, CELLS)


def filter_kernel(
    n, rows, dom, wav, pot, amat_hbm, fil_out, g_out,
    amat, ext0, ext1, ext2, ext3, last, potb, diag, fil, acc, gsend, grecv, gback, gfin,
    in_send, in_recv, pot_send, pot_recv, halo_send, halo_recv,
    out_send, out_recv, load, store, a_send, a_recv, b_send, b_recv,
):
    me = lax.axis_index("gz")
    ext = (ext0, ext1, ext2, ext3)
    planes = wav.shape[0]
    own = 2 * planes
    quad = me // 4
    r = me % 4
    half = r // 2
    core = r % 2
    link = quad * 2 + core
    lower_dev = ((link - 1) // 2) * 4 + 2 * half + (link + 1) % 2
    upper_dev = ((link + 1) // 2) * 4 + 2 * half + (link + 1) % 2
    has_lower = link > 0
    has_upper = link < n // 2 - 1

    barrier = pltpu.get_barrier_semaphore()

    @pl.loop(1, n)
    def _(off):
        pl.semaphore_signal(
            barrier, inc=1, device_id={"gz": (me + off) % n}, device_id_type=MESH
        )

    amat_copy = pltpu.make_async_copy(amat_hbm, amat, load)
    amat_copy.start()

    @pl.when(jnp.logical_not(has_lower))
    def _():
        for step in range(DEGREE):
            ext[step][0:HALO] = jnp.zeros((HALO, CELLS, PANEL), jnp.bfloat16)

    @pl.when(jnp.logical_not(has_upper))
    def _():
        for step in range(DEGREE):
            ext[step][HALO + own : HALO + own + HALO] = jnp.zeros(
                (HALO, CELLS, PANEL), jnp.bfloat16
            )

    pl.semaphore_wait(barrier, n - 1)

    first = quad * 4 + core * 2
    marks = [dom[jnp.clip(first + b, 0, n - 1)] for b in (-1, 0, 1, 2)]
    ones = [
        jnp.where((marks[0] == marks[1]) & has_lower, 1.0, 0.0).astype(jnp.float32),
        jnp.where(marks[1] == marks[2], 1.0, 0.0).astype(jnp.float32),
        jnp.where((marks[2] == marks[3]) & has_upper, 1.0, 0.0).astype(jnp.float32),
    ]
    mid = ones[1]
    far = jnp.where(core == 0, ones[0], ones[2])
    near = jnp.where(core == 0, ones[2], ones[0])

    slot = r % 2
    starts = (HALO * slot, HALO * (1 - slot))

    def in_copy(h, piece, remote):
        start = starts[piece]
        src = wav.at[pl.ds(start, HALO), :, h * PANEL : (h + 1) * PANEL]
        dst = ext0.at[pl.ds(HALO + planes * slot + start, HALO)]
        if remote:
            return pltpu.make_async_remote_copy(
                src_ref=src, dst_ref=dst,
                send_sem=in_send.at[h, piece], recv_sem=in_recv.at[slot, piece],
                device_id={"gz": quad * 4 + 2 * h + half}, device_id_type=MESH,
            )
        return pltpu.make_async_copy(src, dst, in_recv.at[slot, piece])

    def pot_copy(h, remote):
        if remote:
            return pltpu.make_async_remote_copy(
                src_ref=pot, dst_ref=potb.at[slot],
                send_sem=pot_send.at[h], recv_sem=pot_recv.at[slot],
                device_id={"gz": quad * 4 + 2 * h + half}, device_id_type=MESH,
            )
        return pltpu.make_async_copy(pot, potb.at[slot], pot_recv.at[slot])

    for h in (0, 1):
        away = quad * 4 + 2 * h + half != me

        @pl.when(away)
        def _(h=h):
            in_copy(h, 0, True).start()
            pot_copy(h, True).start()
            in_copy(h, 1, True).start()

        @pl.when(jnp.logical_not(away))
        def _(h=h):
            in_copy(h, 0, False).start()
            pot_copy(h, False).start()
            in_copy(h, 1, False).start()

    def in_wait(which, piece):
        start = HALO * which if piece == 0 else HALO * (1 - which)
        dst = ext0.at[pl.ds(HALO + planes * which + start, HALO)]
        pltpu.make_async_copy(dst, dst, in_recv.at[which, piece]).wait()

    def down_copy(step, piece):
        start, count = ((0, 2), (2, 1))[piece]
        return pltpu.make_async_remote_copy(
            src_ref=ext[step].at[pl.ds(HALO + start, count)],
            dst_ref=ext[step].at[pl.ds(HALO + own + start, count)],
            send_sem=halo_send.at[step, 0, piece], recv_sem=halo_recv.at[step, 0, piece],
            device_id={"gz": lower_dev}, device_id_type=MESH,
        )

    def up_copy(step, piece):
        start, count = ((1, 2), (0, 1))[piece]
        return pltpu.make_async_remote_copy(
            src_ref=ext[step].at[pl.ds(own + start, count)],
            dst_ref=ext[step].at[pl.ds(start, count)],
            send_sem=halo_send.at[step, 1, piece], recv_sem=halo_recv.at[step, 1, piece],
            device_id={"gz": upper_dev}, device_id_type=MESH,
        )

    def send_far(step, pieces=(0, 1)):
        @pl.when((core == 0) & has_lower)
        def _():
            for piece in pieces:
                down_copy(step, piece).start()

        @pl.when((core == 1) & has_upper)
        def _():
            for piece in pieces:
                up_copy(step, piece).start()

    def send_near(step):
        @pl.when(core == 0)
        def _():
            for piece in (0, 1):
                up_copy(step, piece).start()

        @pl.when(core == 1)
        def _():
            for piece in (0, 1):
                down_copy(step, piece).start()

    def wait_far(step):
        @pl.when((core == 0) & has_lower)
        def _():
            for piece in (0, 1):
                up_copy(step, piece).wait_recv()

        @pl.when((core == 1) & has_upper)
        def _():
            for piece in (0, 1):
                down_copy(step, piece).wait_recv()

    def wait_near(step):
        @pl.when(core == 0)
        def _():
            for piece in (0, 1):
                down_copy(step, piece).wait_recv()

        @pl.when(core == 1)
        def _():
            for piece in (0, 1):
                up_copy(step, piece).wait_recv()

    in_wait(core, 0)
    send_far(0)
    in_wait(1 - core, 0)
    send_near(0)
    amat_copy.wait()

    for which in (0, 1):
        pltpu.make_async_copy(potb.at[which], potb.at[which], pot_recv.at[which]).wait()

        @pl.loop(0, planes)
        def _(i, which=which):
            row = SCALE * (potb[which, pl.ds(i, 1), :] - (CSHIFT + 1.5 * COEF[0]))
            diag[planes * which + i] = jnp.broadcast_to(row, (PANEL, CELLS)).T

    in_wait(0, 1)
    in_wait(1, 1)

    def inward(t):
        return jnp.where(core == 0, t, own - 1 - t)

    def z_terms(source, t, at):
        total = None
        for k in (1, 2, 3):
            weight = -0.5 * SCALE * COEF[k]
            outer, inner = (
                source[HALO + inward(t + s), at, :].astype(jnp.float32) for s in (-k, k)
            )
            if t - k < 0:
                term = outer * (far * weight) + inner * weight
            elif t < planes <= t + k:
                term = outer * weight + inner * (mid * weight)
            elif t - k < planes <= t:
                term = outer * (mid * weight) + inner * weight
            elif t + k >= own:
                term = outer * weight + inner * (near * weight)
            else:
                term = (outer + inner) * weight
            total = term if total is None else total + term
        return total

    def update(step, first, second):
        source = ext[step]
        pair = jnp.concatenate(
            [source[HALO + inward(first)], source[HALO + inward(second)]], axis=1
        )

        def products(tile):
            return jnp.dot(amat[tile], pair, preferred_element_type=jnp.float32)

        tiles = CELLS // TILE
        ready = products(0)
        for tile in range(tiles):
            at = slice(tile * TILE, (tile + 1) * TILE)
            both = ready
            if tile + 1 < tiles:
                ready = products(tile + 1)
            image = both[:TILE] + both[TILE:]
            for place, t in enumerate((first, second)):
                plane = inward(t)
                value = image[:, place * PANEL : (place + 1) * PANEL]
                centre = source[HALO + plane, at, :].astype(jnp.float32)
                value = value + diag[plane, at, :] * centre + z_terms(source, t, at)
                if step == 0:
                    value = value * 0.5
                else:
                    value = value - ext[step - 1][HALO + plane, at, :].astype(jnp.float32)
                value = value.astype(jnp.bfloat16)
                if step < DEGREE - 1:
                    ext[step + 1][HALO + plane, at, :] = value
                else:
                    last[plane, at, :] = value

    def out_copy(part, remote):
        which, piece = part // 2, part % 2
        src = last.at[pl.ds(HALO * part, HALO)]
        dst = fil.at[half, pl.ds(HALO * piece, HALO)]
        if remote:
            return pltpu.make_async_remote_copy(
                src_ref=src, dst_ref=dst,
                send_sem=out_send.at[part], recv_sem=out_recv.at[half, piece],
                device_id={"gz": quad * 4 + 2 * core + which}, device_id_type=MESH,
            )
        return pltpu.make_async_copy(src, dst, out_recv.at[half, piece])

    def send_out(t_part):
        part = jnp.where(core == 0, t_part, 3 - t_part)
        away = quad * 4 + 2 * core + part // 2 != me

        @pl.when(away)
        def _():
            out_copy(part, True).start()

        @pl.when(jnp.logical_not(away))
        def _():
            out_copy(part, False).start()

    def update_pairs(step, start, count):
        for j in range(count):
            update(step, start + 2 * j, start + 2 * j + 1)

    for step in range(DEGREE):
        final = step == DEGREE - 1
        wait_near(step)
        update_pairs(step, own - 4, 2)
        if final:
            send_out(3)
        else:
            send_near(step + 1)
        update_pairs(step, own - 8, 2)
        if final:
            send_out(2)
        wait_far(step)
        update_pairs(step, 0, 1)
        if not final:
            send_far(step + 1, (0,))
        update_pairs(step, 2, 1)
        if final:
            send_out(0)
            send_out(1)
        else:
            send_far(step + 1, (1,))

    def out_wait(h, piece):
        dst = fil.at[h, pl.ds(HALO * piece, HALO)]
        pltpu.make_async_copy(dst, dst, out_recv.at[h, piece]).wait()

    def store_copy(h, piece):
        return pltpu.make_async_copy(
            fil.at[h, pl.ds(HALO * piece, HALO)],
            fil_out.at[pl.ds(HALO * piece, HALO), :, h * PANEL : (h + 1) * PANEL],
            store.at[h, piece],
        )

    acc[...] = jnp.zeros_like(acc)
    for piece in (1 - half, half):
        for h in (0, 1):
            out_wait(h, piece)
            store_copy(h, piece).start()

        @pl.loop(0, HALO)
        def _(i, piece=piece):
            at = HALO * piece + i
            both = jnp.concatenate([fil[0, at], fil[1, at]], axis=1)
            gram = lax.dot_general(
                both, both, (((0,), (0,)), ((), ())), preferred_element_type=jnp.float32
            )
            acc[0] += gram[0:PANEL, 0:PANEL]
            acc[1] += gram[0:PANEL, PANEL:]
            acc[2] += gram[PANEL:, PANEL:]

    def exchange(make, src, dst, send, recv):
        def copy(target, origin):
            return pltpu.make_async_remote_copy(
                src_ref=src.at[target], dst_ref=dst.at[origin],
                send_sem=send.at[target], recv_sem=recv.at[origin],
                device_id={"gz": target}, device_id_type=MESH,
            )

        @pl.loop(1, n)
        def _(off):
            there = (me + off) % n
            src[there] = make(there)
            copy(there, me).start()

        dst[me] = make(me)

        @pl.loop(1, n)
        def _(off):
            copy((me + off) % n, (me + off) % n).wait_recv()

    def row_chunk(j):
        return acc[:, pl.ds(pl.multiple_of(j * rows, rows), rows), :]

    def domain_mean(j):
        mark = dom[j]

        def add(i, sums):
            total, blocks = sums
            same = jnp.where(dom[i] == mark, 1.0, 0.0).astype(jnp.float32)
            return total + same * grecv[i], blocks + same

        zero = jnp.zeros((3, rows, PANEL), jnp.float32)
        total, blocks = lax.fori_loop(
            0, n, add, (zero, jnp.float32(0.0)), unroll=min(n, 16)
        )
        return total / jnp.full((3, rows, PANEL), blocks * (planes * CELLS), jnp.float32)

    exchange(row_chunk, gsend, grecv, a_send, a_recv)
    exchange(domain_mean, gback, gfin, b_send, b_recv)

    @pl.loop(0, n)
    def _(j):
        g_out[:, pl.ds(pl.multiple_of(j * rows, rows), rows), :] = gfin[j]

    for h in (0, 1):
        away = quad * 4 + 2 * h + half != me

        @pl.when(away)
        def _(h=h):
            in_copy(h, 0, True).wait_send()
            pot_copy(h, True).wait_send()
            in_copy(h, 1, True).wait_send()

        back = quad * 4 + 2 * core + h != me

        @pl.when(back)
        def _(h=h):
            out_copy(2 * h, True).wait_send()
            out_copy(2 * h + 1, True).wait_send()

        store_copy(h, 0).wait()
        store_copy(h, 1).wait()

    for step in range(DEGREE):

        @pl.when(has_lower)
        def _(step=step):
            for piece in (0, 1):
                down_copy(step, piece).wait_send()

        @pl.when(has_upper)
        def _(step=step):
            for piece in (0, 1):
                up_copy(step, piece).wait_send()

    @pl.loop(1, n)
    def _(off):
        there = (me + off) % n
        pltpu.make_async_copy(gsend.at[there], gsend.at[there], a_send.at[there]).wait()
        pltpu.make_async_copy(gback.at[there], gback.at[there], b_send.at[there]).wait()


def filtered_and_gram(n, waves, potential, domain_of):
    planes = waves.shape[0]
    bands = waves.shape[2]
    rows = PANEL // n
    own = 2 * planes
    vmem = pl.BlockSpec(memory_space=pltpu.VMEM)
    smem = pl.BlockSpec(memory_space=pltpu.SMEM)
    hbm = pl.BlockSpec(memory_space=pl.ANY)
    dma = pltpu.SemaphoreType.DMA
    wide = pltpu.VMEM((own + 2 * HALO, CELLS, PANEL), jnp.bfloat16)
    chunk = pltpu.VMEM((n, 3, rows, PANEL), jnp.float32)
    return pl.pallas_call(
        functools.partial(filter_kernel, n, rows),
        out_shape=(
            jax.ShapeDtypeStruct((planes, CELLS, bands), jnp.bfloat16),
            jax.ShapeDtypeStruct((3, PANEL, PANEL), jnp.float32),
        ),
        in_specs=[smem, hbm, hbm, hbm],
        out_specs=(hbm, vmem),
        scratch_shapes=[
            pltpu.VMEM((CELLS // TILE, 2 * TILE, CELLS), jnp.bfloat16),
            wide, wide, wide, wide,
            pltpu.VMEM((own, CELLS, PANEL), jnp.bfloat16),
            pltpu.VMEM((2, planes, CELLS), jnp.float32),
            pltpu.VMEM((own, CELLS, PANEL), jnp.float32),
            pltpu.VMEM((2, planes, CELLS, PANEL), jnp.bfloat16),
            pltpu.VMEM((3, PANEL, PANEL), jnp.float32),
            chunk, chunk, chunk, chunk,
            dma((2, 2)), dma((2, 2)), dma((2,)), dma((2,)),
            dma((DEGREE, 2, 2)), dma((DEGREE, 2, 2)), dma((4,)), dma((2, 2)), dma, dma((2, 2)),
            dma((n,)), dma((n,)), dma((n,)), dma((n,)),
        ],
        compiler_params=pltpu.CompilerParams(
            collective_id=0, has_side_effects=True, vmem_limit_bytes=58 * 2**20
        ),
        cost_estimate=pl.CostEstimate(
            flops=8 * 10**9, bytes_accessed=5 * 10**6, transcendentals=0
        ),
        name="filter_gram",
    )(domain_of, waves, potential, jnp.asarray(plane_matrix()))


BLOCK = 16


def exact(a, b, contract=((1,), (0,))):
    return lax.dot_general(
        a, b, (contract, ((), ())),
        precision=lax.Precision.HIGHEST, preferred_element_type=jnp.float32,
    )


def inverse_factor(gram, beside=None):
    row = lax.broadcasted_iota(jnp.int32, (BLOCK, PANEL), 0)
    lane = lax.broadcasted_iota(jnp.int32, (BLOCK, PANEL), 1)
    rest = gram
    result = []
    for start in range(0, PANEL, BLOCK):
        if beside is not None:
            beside(start // BLOCK, PANEL // BLOCK)
        top = rest[:BLOCK]
        inside = (lane >= start) & (lane < start + BLOCK)
        pivot_columns = [
            jnp.broadcast_to(top[:, start + j : start + j + 1], (BLOCK, PANEL))
            for j in range(BLOCK)
        ]
        top = jnp.where(inside, jnp.where(lane - start == row, 1.0, 0.0), top)
        scale = jnp.zeros((BLOCK, PANEL), jnp.float32)
        for j in range(BLOCK):
            pivot = jnp.broadcast_to(pivot_columns[j][j : j + 1], (BLOCK, PANEL))
            over = 1.0 / pivot
            scale = jnp.where(row == j, over, scale)
            if j == BLOCK - 1:
                break
            column = jnp.where(row > j, pivot_columns[j], 0.0)
            for later in range(j + 1, BLOCK):
                product = column * jnp.broadcast_to(
                    pivot_columns[later][j : j + 1], (BLOCK, PANEL)
                )
                pivot_columns[later] = pivot_columns[later] - product * over
            top = top - (column * jnp.broadcast_to(top[j : j + 1], (BLOCK, PANEL))) * over
        end = start + BLOCK
        result.append(jnp.where(lane < end, top * jnp.sqrt(scale), 0.0))
        if end < PANEL:
            ratio = jnp.where(lane >= end, top * scale, 0.0)
            change = exact(ratio, top, ((0,), (0,)))[end:]
            below = lax.broadcasted_iota(jnp.int32, (PANEL - end, PANEL), 1)
            keep = jnp.where((below >= start) & (below < end), 0.0, rest[BLOCK:])
            rest = keep - change
    return jnp.concatenate(result, axis=0)


def whiten_kernel(fil_hbm, sums, out_hbm, fil, out, reduced, load, store):
    load_copy = pltpu.make_async_copy(fil_hbm, fil, load)
    load_copy.start()
    g00, g01, g11 = sums[0], sums[1], sums[2]
    w0 = inverse_factor(g00).astype(jnp.bfloat16)
    w0f = w0.astype(jnp.float32)
    corr = exact(w0f, g01)
    corr_r = corr.astype(jnp.bfloat16)
    cf = corr_r.astype(jnp.float32)
    middle = exact(exact(exact(w0f, g00), w0f, ((1,), (1,))), cf) - corr
    gram1 = g11 + exact(cf, middle, ((0,), (0,))) - exact(corr, cf, ((0,), (0,)))
    load_copy.wait()
    planes = fil.shape[0]

    def times(a, b, contract):
        return lax.dot_general(a, b, (contract, ((), ())), preferred_element_type=jnp.float32)

    chunks = [(i, t * TILE) for i in range(planes) for t in range(CELLS // TILE)]

    def reduce_some(place, blocks):
        share = -(-len(chunks) // blocks)
        for i, start in chunks[place * share : (place + 1) * share]:
            at = slice(start, start + TILE)
            e0 = times(fil[i, at, :PANEL], w0, ((1,), (1,))).astype(jnp.bfloat16)
            out[i, at, :PANEL] = e0
            b1 = fil[i, at, PANEL:].astype(jnp.float32)
            left = (b1 - times(e0, corr_r, ((1,), (0,)))).astype(jnp.bfloat16)
            reduced[i, at, :] = left

    w1 = inverse_factor(gram1, reduce_some).astype(jnp.bfloat16)

    @pl.loop(0, planes)
    def _(i):
        out[i, :, PANEL:] = times(reduced[i], w1, ((1,), (1,))).astype(jnp.bfloat16)
        pltpu.make_async_copy(out.at[i], out_hbm.at[i], store.at[i]).start()

    @pl.loop(0, fil.shape[0])
    def _(i):
        pltpu.make_async_copy(out.at[i], out_hbm.at[i], store.at[i]).wait()


def shards(waves, potential, domain_of):
    n = lax.axis_size("gz")
    planes = waves.shape[0]
    bands = waves.shape[3]
    filtered, sums = filtered_and_gram(
        n, waves.reshape(planes, CELLS, bands), potential, domain_of
    )
    vmem = pl.BlockSpec(memory_space=pltpu.VMEM)
    hbm = pl.BlockSpec(memory_space=pl.ANY)
    orbitals = pl.pallas_call(
        whiten_kernel,
        out_shape=jax.ShapeDtypeStruct((planes, CELLS, bands), jnp.bfloat16),
        in_specs=[hbm, vmem],
        out_specs=hbm,
        scratch_shapes=[
            pltpu.VMEM((planes, CELLS, bands), jnp.bfloat16),
            pltpu.VMEM((planes, CELLS, bands), jnp.bfloat16),
            pltpu.VMEM((planes, CELLS, PANEL), jnp.bfloat16),
            pltpu.SemaphoreType.DMA,
            pltpu.SemaphoreType.DMA((planes,)),
        ],
        compiler_params=pltpu.CompilerParams(vmem_limit_bytes=58 * 2**20),
        cost_estimate=pl.CostEstimate(
            flops=4 * 10**8, bytes_accessed=4 * 10**6, transcendentals=0
        ),
        name="whiten",
    )(filtered, sums)
    return orbitals.reshape(planes, NY, NX, bands)


def solution(mesh):
    return jax.shard_map(
        shards,
        mesh=mesh,
        in_specs=(P(("groups", "gz"), None, None, None), P(("groups", "gz"), None), P("groups")),
        out_specs=P(("groups", "gz"), None, None, None),
        check_vma=False,
    )
```
